1024 devices in a mesh: gx: 16 (over x, core), gy: 64 (over y, z).
Axes of the slice: x: 8, y: 8, z: 8, core: 2. Of those that a mesh axis runs over, the one named last changes fastest.
Arguments:
- displacement: float32 [3, 8, 512, 2048], P(None, None, 'gy', 'gx'), may hold values from -6 to 6
- velocity: float32 [3, 8, 512, 2048], P(None, None, 'gy', 'gx'), may hold values from -12 to 12
- body_force: float32 [3, 8, 512, 2048], P(None, None, 'gy', 'gx'), may hold values from -12 to 12
- modulus: float32 [8, 512, 2048], P(None, 'gy', 'gx'), may hold values from 0.5 to 2
- damage_bits: int32 [2, 8, 512, 2048], P(None, None, 'gy', 'gx'), may hold values from 0 to 255, as said below
Outputs:
- final_displacement: float32 [3, 8, 512, 2048], P(None, None, 'gy', 'gx')
- final_velocity: float32 [3, 8, 512, 2048], P(None, None, 'gy', 'gx')
The draws below stay inside these ranges and needn't reach their ends.
Inputs may be any that keep to these rules, and one draw needn't show every extreme that they name: `damage_bits`: only bits 0 to 7 may be set.
All inputs are finite; a program needn't handle non-finite values.
Results may differ from the reference program's by a relative error of at most 0.015.
Values sent between devices are 32-bit elements; how exact they have to be, the bound alone decides.
A program may use at most 32 MiB of HBM per device.

```python
import math
import jax
import jax.numpy as jnp

NZ = 8
ITERS = 4
NX = 2048
NY = 512


def draw_velocity(key, part):
    key = jax.random.fold_in(key, 11)
    column_ramp = (jnp.arange(NX, dtype=jnp.float32) / NX)[None, None, None, :]
    drawn = jnp.clip(jax.random.normal(key, (3, NZ, NY, NX), jnp.float32), -4.0, 4.0) * (1.0 + 2.0 * column_ramp)
    return drawn


def draw_damage_bits(key, part):
    key = jax.random.fold_in(key, 5)
    packed = jnp.zeros((2, NZ, NY, NX), jnp.int32)
    for number in range(8):
        bond_key = jax.random.fold_in(key, number)
        broken = (jax.random.randint(bond_key, (2, NZ, NY, NX), 0, 8) == 0).astype(jnp.int32)
        packed = packed + broken * 2 ** number
    point_count = NZ * NY * NX
    chosen = jax.random.randint(jax.random.fold_in(key, 99), (), 0, point_count)
    point_ids = jnp.arange(point_count, dtype=jnp.int32).reshape((1, NZ, NY, NX))
    packed = jnp.where(point_ids == chosen, 255, packed)
    packed = jnp.where(point_ids == (chosen + 1) % point_count, 0, packed)
    return packed


def shard_levels(own_key, shape, split, low, high):
    loudness, own = 1.0, jax.random.fold_in(own_key, 6)
    for position, shards_of in split:
        heights = jnp.exp(jax.random.uniform(jax.random.fold_in(own, position), (shards_of,), jnp.float32, low / len(split), high / len(split)))
        loudness = loudness * jnp.repeat(heights, shape[position] // shards_of).reshape([-1 if axis == position else 1 for axis in range(len(shape))])
    return loudness


def centred(rng, shape, width, reach, split=(), held_as=jnp.bfloat16):
    values = jax.random.normal(rng, shape, jnp.float32) * width
    if len(split) > 0:
        values = shard_levels(rng, shape, split, -0.22, 0.18) * values
    return jnp.clip(values, min=-reach, max=reach).astype(held_as)


def setup_inputs(seed: int = 0) -> dict:
    arg_keys = jax.random.split(jax.random.key(seed), 6)
    displacement = centred(arg_keys[0], (3, NZ, NY, NX), 1.0, 6.0, ((2, 64), (3, 16)), jnp.float32)
    velocity = draw_velocity(jax.random.fold_in(arg_keys[5], 71), 0)
    body_force = centred(arg_keys[2], (3, NZ, NY, NX), 2.0, 12.0, ((2, 64), (3, 16)), jnp.float32)
    modulus = jnp.clip(jnp.exp(math.log(2.0) - 1.3862944 * jax.random.uniform(arg_keys[3], (NZ, NY, NX), jnp.float32) ** shard_levels(arg_keys[3], (NZ, NY, NX), ((1, 64), (2, 16)), -0.2, 0.2)), 0.5, 2.0)
    damage_bits = draw_damage_bits(jax.random.fold_in(arg_keys[5], 71), 0)
    return {"displacement": displacement, "velocity": velocity, "body_force": body_force, "modulus": modulus, "damage_bits": damage_bits}


def half_offsets():
    result = []
    for step_x in range(-2, 3):
        for step_y in range(-2, 3):
            for step_z in range(-2, 3):
                length_sq = step_x * step_x + step_y * step_y + step_z * step_z
                leading = step_x if step_x != 0 else step_y if step_y != 0 else step_z
                if 0 < length_sq <= 4 and leading > 0:
                    result.append((step_x, step_y, step_z))
    return result

def mass_scale():
    return 2.0 * sum((1.0 / math.sqrt(entry[0] * entry[0] + entry[1] * entry[1] + entry[2] * entry[2]) for entry in half_offsets()))

def internal(vector_field, modulus, damage_bits):
    layer_count, row_count, column_count = modulus.shape
    padded = jnp.pad(vector_field, ((0, 0), (2, 2), (2, 2), (2, 2)))
    modulus_pad = jnp.pad(modulus, 2)
    inside_pad = jnp.pad(jnp.ones_like(modulus), 2)
    forces = jnp.zeros_like(padded)
    interior = (slice(None), slice(2, 2 + layer_count), slice(2, 2 + row_count), slice(2, 2 + column_count))
    for number, step in enumerate(half_offsets()):
        window = (slice(2 + step[2], 2 + step[2] + layer_count), slice(2 + step[1], 2 + step[1] + row_count), slice(2 + step[0], 2 + step[0] + column_count))
        partner = padded[(slice(None),) + window]
        stretch = step[0] * (partner[0] - vector_field[0]) + step[1] * (partner[1] - vector_field[1]) + step[2] * (partner[2] - vector_field[2])
        broken = jnp.bitwise_and(jnp.right_shift(damage_bits[number // 8], number % 8), 1).astype(jnp.float32)
        length = math.sqrt(step[0] * step[0] + step[1] * step[1] + step[2] * step[2])
        stiffness = 0.5 * (modulus + modulus_pad[window]) * (1.0 - broken) * inside_pad[window] / (length * length * length)
        magnitude = stiffness * stretch
        bond_pull = jnp.stack([magnitude * step[0], magnitude * step[1], magnitude * step[2]])
        forces = forces.at[interior].add(bond_pull)
        forces = forces.at[(slice(None),) + window].add(-bond_pull)
    return forces[interior]

def reference(displacement, velocity, body_force, modulus, damage_bits):
    fictive_mass = mass_scale()
    forces = internal(displacement, modulus, damage_bits)
    current = displacement
    velocity_now = velocity
    for iteration in range(ITERS):
        change = internal(velocity_now, modulus, damage_bits)
        if iteration > 0:
            forces = forces + change
        numerator = -jnp.sum(velocity_now * change) / fictive_mass
        denominator = jnp.sum(velocity_now * velocity_now)
        damping = 2.0 * jnp.sqrt(numerator / (denominator + 1e-06))
        velocity_now = ((2.0 - damping) * velocity_now + 2.0 * (forces + body_force) / fictive_mass) / (2.0 + damping)
        current = current + velocity_now
    return (current, velocity_now)
```

```python
import functools
import math

import jax
import jax.numpy as jnp
from jax import lax
from jax.experimental import pallas as pl
from jax.experimental.pallas import tpu as pltpu
from jax.sharding import PartitionSpec as P

ITERS = 4
STEPS = ITERS
NZ, NY, NX = 8, 8, 128
GX, GY, GZ = 16, 8, 8
MESH = pl.DeviceIdType.MESH
F32 = jnp.float32


def half_offsets():
    result = []
    for step_x in range(-2, 3):
        for step_y in range(-2, 3):
            for step_z in range(-2, 3):
                length_sq = step_x * step_x + step_y * step_y + step_z * step_z
                leading = step_x if step_x != 0 else step_y if step_y != 0 else step_z
                if 0 < length_sq <= 4 and leading > 0:
                    result.append((step_x, step_y, step_z))
    return result


HALF = half_offsets()
FULL = [(entry, number, 1) for number, entry in enumerate(HALF)] + [
    (tuple(-part for part in entry), number, -1) for number, entry in enumerate(HALF)
]
BOND = {entry: place for place, (entry, _, _) in enumerate(FULL)}
FICTIVE_MASS = 2.0 * sum(1.0 / math.sqrt(a * a + b * b + c * c) for a, b, c in HALF)

SIDES = [(-1, 0), (1, 0), (-1, -1), (1, -1), (-1, 1), (1, 1)]


def hops(distance, count):
    return min(distance % count, -distance % count)


X_PARTNERS = sorted(range(1, GX), key=lambda d: -hops(d, GX))
YZ_PARTNERS = sorted(
    [(dy, dz) for dy in range(GY) for dz in range(GZ) if dy or dz],
    key=lambda d: -(hops(d[0], GY) + hops(d[1], GZ)),
)

VV = [18, 0, 1, 6, 7, 12]
GG = [3, 8, 9, 14, 15, 19]
VG = [4, 5, 10, 11, 16, 17]
SLOTS = 24


def kernel(
    u_hbm, v_hbm, body_hbm, mod_hbm, bits_hbm, u_out, v_out,
    raw_u, raw_v, raw_body, raw_mod, raw_bits,
    field, static, ahead, behind, ahead2, behind2, stiff, sides_static, last,
    edge_out, edge_in, inner_in, static_in, moments, row_out, row_x, row_yz,
    load_sem, y_send, y_recv, e_send, e_recv, i_send, i_recv, s_send, s_recv, sy_send, sy_recv,
    rx_send, rx_recv, ryz_send, ryz_recv,
):
    gx, gy = lax.axis_index("gx"), lax.axis_index("gy")
    part_y, part_z = gy // GZ, gy % GZ

    def near(dx, dy):
        return ((gx + dx + GX) % GX, (gy + dy + GY * GZ) % (GY * GZ))

    x_partners = [((gx + d) % GX, gy) for d in X_PARTNERS]
    yz_partners = [
        (gx, ((part_y + dy) % GY) * GZ + (part_z + dz) % GZ) for dy, dz in YZ_PARTNERS
    ]
    near_all = [(dx, dy) for dx in (-1, 0, 1) for dy in (-1, 0, 1) if dx or dy]
    barrier = pltpu.get_barrier_semaphore()
    greeted = [near(dx, dy) for dx, dy in near_all] + x_partners + yz_partners
    for device in greeted:
        pl.semaphore_signal(barrier, inc=1, device_id=device, device_id_type=MESH)

    loads = [
        pltpu.make_async_copy(source, target, load_sem.at[place])
        for place, (source, target) in enumerate(
            [(u_hbm, raw_u), (v_hbm, raw_v), (mod_hbm, raw_mod), (bits_hbm, raw_bits), (body_hbm, raw_body)]
        )
    ]
    for load in loads:
        load.start()

    lane = lax.broadcasted_iota(jnp.int32, (NZ, NX), 1)
    layer = lax.broadcasted_iota(jnp.int32, (NZ, NX), 0)

    def lanes_on(value, amount):
        return pltpu.roll(value, (-amount) % NX, axis=1)

    def layers_on(value, amount):
        return value if amount == 0 else pltpu.roll(value, (-amount) % NZ, axis=0)

    def pack(values):
        total = jnp.zeros((NZ, NX), F32)
        for place, value in enumerate(values):
            total = jnp.where(lane // 4 == place, pltpu.roll(value, (4 * place + 2) % NX, axis=1), total)
        return total

    def joined(left, right):
        return jnp.where(lane % 4 < 2, left, right)

    def rim(both, place):
        return pltpu.roll(both, (2 * NX - 4 * place - 2) % NX, axis=1)

    def plus(value, halo, amount):
        if amount > 0:
            return lanes_on(jnp.where(lane < amount, halo, value), amount)
        return lanes_on(jnp.where(lane >= NX + amount, halo, value), amount)

    def remote(source, target, send, recv, device):
        return pltpu.make_async_remote_copy(
            src_ref=source, dst_ref=target, send_sem=send, recv_sem=recv,
            device_id=device, device_id_type=MESH,
        )

    def y_copies(step):
        return [
            remote(field.at[step, :, :, 9], field.at[step, :, :, 1], y_send.at[step, 0], y_recv.at[step, 0], near(0, 1)),
            remote(field.at[step, :, :, 2], field.at[step, :, :, 10], y_send.at[step, 1], y_recv.at[step, 1], near(0, -1)),
            remote(field.at[step, :, 1, 8], field.at[step, :, 1, 0], y_send.at[step, 2], y_recv.at[step, 2], near(0, 1)),
            remote(field.at[step, :, 1, 3], field.at[step, :, 1, 11], y_send.at[step, 3], y_recv.at[step, 3], near(0, -1)),
        ]

    def static_y_copies():
        return [
            remote(static.at[:, 9], static.at[:, 1], sy_send.at[0], sy_recv.at[0], near(0, 1)),
            remote(static.at[:, 2], static.at[:, 10], sy_send.at[1], sy_recv.at[1], near(0, -1)),
            remote(static.at[0:2, 8], static.at[0:2, 0], sy_send.at[2], sy_recv.at[2], near(0, 1)),
            remote(static.at[0:1, 3], static.at[0:1, 11], sy_send.at[3], sy_recv.at[3], near(0, -1)),
        ]

    def edge_copies(step, source, target, send, recv, count):
        return [
            remote(source, target.at[step, place], send.at[step, place], recv.at[step, place], near(-dx, -dy))
            for place, (dx, dy) in reversed(list(enumerate(SIDES[:count])))
        ]

    def boundary_copies(step):
        return edge_copies(step, edge_out.at[step, 0], edge_in, e_send, e_recv, 6)

    def inner_copies(step):
        return edge_copies(step, edge_out.at[step, 1], inner_in, i_send, i_recv, 2)

    def static_copies():
        return edge_copies(0, sides_static, static_in, s_send, s_recv, 6)

    BOUNDARY = (0, 1, 6, 7)
    INNER = (2, 3, 4, 5)

    def pack_rows(step, rows):
        return pack([field[step, f, c, 2 + y] for y in rows for f in range(2) for c in range(3)])

    for load in loads[:4]:
        load.wait()
    for y in range(NY):
        turned = pl.ds(y, NZ, stride=NY)
        for c in range(3):
            field[0, 0, c, 2 + y] = raw_u[c, turned, :]
            field[0, 1, c, 2 + y] = raw_v[c, turned, :]
        static[0, 2 + y] = raw_mod[turned, :]
        for c in range(2):
            static[1 + c, 2 + y] = raw_bits[c, turned, :].astype(F32)
    edge_out[0, 0] = pack_rows(0, BOUNDARY)
    edge_out[0, 1] = pack_rows(0, INNER)
    sides_static[...] = pack([static[c, 2 + y] for y in range(NY) for c in range(3)])

    pl.semaphore_wait(barrier, len(greeted))
    for copy in static_y_copies() + static_copies() + y_copies(0) + boundary_copies(0) + inner_copies(0):
        copy.start()
    loads[4].wait()

    for copy in static_y_copies() + static_copies():
        copy.wait_recv()
    edge = {-1: joined(static_in[0, 2], static_in[0, 3]), 0: joined(static_in[0, 0], static_in[0, 1]), 1: joined(static_in[0, 4], static_in[0, 5])}
    for y in range(-1, NY + 1):
        side = -1 if y < 0 else 1 if y >= NY else 0
        row = y - side * NY
        for c in range(3):
            value, halo = static[c, 2 + y], rim(edge[side], 3 * row + c)
            if c == 0:
                ahead[1, 0, 0, 1 + y] = plus(value, halo, 1)
            behind[1, 0, c, 1 + y] = plus(value, halo, -1)
            if side == 0 and c == 0:
                ahead2[1, 0, y] = plus(value, halo, 2)
            if side == 0 and c != 1:
                behind2[1, c // 2, y] = plus(value, halo, -2)

    column_on = {}
    for a in range(-2, 3):
        on = jnp.logical_and(
            jnp.logical_or(gx > 0, lane + a >= 0), jnp.logical_or(gx < GX - 1, lane + a < NX)
        )
        column_on[a] = on
    layer_on = {c: jnp.logical_and(layer + c >= 0, layer + c < NZ) for c in range(-2, 3)}
    weight = {}
    for a, b, c in BOND:
        if (a, c) not in weight:
            weight[a, c] = jnp.logical_and(column_on[a], layer_on[c]).astype(F32)

    def stiff_row(y, carry):
        def mod_at(a, b):
            if a == 0:
                return static[0, 2 + y + b]
            if abs(a) == 1:
                return (ahead if a > 0 else behind)[1, 0, 0, 1 + y + b]
            return (ahead2 if a > 0 else behind2)[1, 0, y]

        def bits_at(word, a, b):
            if a == 0:
                value = static[1 + word, 2 + y + b]
            elif a == -1:
                value = behind[1, 0, 1 + word, 1 + y + b]
            else:
                value = behind2[1, 1, y]
            return value.astype(jnp.int32)

        row_on = {}
        for b in range(-2, 3):
            on = jnp.logical_and(
                jnp.logical_or(gy > 0, y + b >= 0), jnp.logical_or(gy < GY * GZ - 1, y + b < NY)
            )
            row_on[b] = jnp.where(on, 1.0, 0.0).astype(F32)
        own = static[0, 2 + y]
        words = {}
        partners = {}
        for place, ((a, b, c), number, sign) in enumerate(FULL):
            if (a, b, c) not in partners:
                partners[a, b, c] = layers_on(mod_at(a, b), c)
            length_sq = a * a + b * b + c * c
            scale = 0.5 / (length_sq * math.sqrt(length_sq))
            if length_sq == 4:
                scale = scale * 4.0
            value = (own + partners[a, b, c]) * (weight[a, c] * (row_on[b] * scale))
            where = (number // 8, a, b) if sign < 0 else (number // 8, 0, 0)
            if where not in words:
                words[where] = bits_at(*where)
            broken = jnp.bitwise_and(words[where], 1 << (number % 8))
            if sign < 0:
                broken = layers_on(broken, c)
            stiff[place, y] = jnp.where(broken == 0, value, 0.0)
        return carry

    lax.fori_loop(0, NY, stiff_row, 0)

    def widen(step, fields, y, edge_side, place):
        for f in fields:
            for c in range(3):
                value, halo = field[step, f, c, 2 + y], rim(edge_side, place + 3 * f + c)
                ahead[0, f, c, 1 + y] = plus(value, halo, 1)
                behind[0, f, c, 1 + y] = plus(value, halo, -1)
                if c == 0 and 0 <= y < NY:
                    ahead2[0, f, y] = plus(value, halo, 2)
                    behind2[0, f, y] = plus(value, halo, -2)

    def row_force(step, f, y):
        own = [field[step, f, c, 2 + y] for c in range(3)]
        force = [jnp.zeros((NZ, NX), F32) for _ in range(3)]

        def bond(a, b, c):
            return stiff[BOND[a, b, c], y]

        for c in (-1, 1, -2, 2):
            force[2] += bond(0, 0, c) * (layers_on(own[2], c) - own[2])
        for b in (-1, 1):
            pair = [None if c == 0 else field[step, f, c, 2 + y + b] for c in range(3)]
            pulls = {}
            for gamma in (-1, 0, 1):
                c = gamma * b
                partner = pair[1] + gamma * pair[2] if gamma else pair[1]
                mine = own[1] + gamma * own[2] if gamma else own[1]
                pulls[gamma] = bond(0, b, c) * (layers_on(partner, c) - mine)
            force[1] += pulls[-1] + pulls[0] + pulls[1]
            force[2] += pulls[1] - pulls[-1]
        for b in (-2, 2):
            force[1] += bond(0, b, 0) * (field[step, f, 1, 2 + y + b] - own[1])
        force[0] += bond(2, 0, 0) * (ahead2[0, f, y] - own[0])
        force[0] += bond(-2, 0, 0) * (behind2[0, f, y] - own[0])
        for beta in (-1, 0, 1):
            mine = own[0] + beta * own[1] if beta else own[0]
            for a in (-1, 1):
                b = a * beta
                source = ahead if a > 0 else behind
                pair = [source[0, f, c, 1 + y + b] for c in range(3)]
                partner = pair[0] + beta * pair[1] if beta else pair[0]
                pulls = {}
                for gamma in (-1, 0, 1):
                    c = gamma * a
                    there = partner + gamma * pair[2] if gamma else partner
                    here = mine + gamma * own[2] if gamma else mine
                    pulls[gamma] = bond(a, b, c) * (layers_on(there, c) - here)
                total = pulls[-1] + pulls[0] + pulls[1]
                force[0] += total
                if beta:
                    force[1] += beta * total
                force[2] += pulls[1] - pulls[-1]
        return own, force

    def dot(first, second):
        return first[0] * second[0] + first[1] * second[1] + first[2] * second[2]

    def rows_pass(step, first_row):
        body_on = jnp.where(step == 0, 1.0, 0.0).astype(F32)

        def row(index, sums):
            y = first_row(index)
            old_g, new_g = row_force(step, 0, y)
            for c in range(3):
                new_g[c] = new_g[c] + body_on * raw_body[c, pl.ds(y, NZ, stride=NY), :]
                field[step + 1, 0, c, 2 + y] = new_g[c]
            old_v, new_v = row_force(step, 1, y)
            for c in range(3):
                field[step + 1, 1, c, 2 + y] = new_v[c]
            terms = [
                dot(old_v, new_v), dot(new_v, new_v), dot(old_g, new_g),
                dot(new_g, new_g), dot(old_v, new_g), dot(new_v, new_g),
            ]
            return tuple(total + term for total, term in zip(sums, terms))

        sums = lax.fori_loop(0, 4, row, (jnp.zeros((NZ, NX), F32),) * 6)
        return sums

    def arrive(step, fields):
        for copy in edge_copies(step, edge_out.at[step, 0], edge_in, e_send, e_recv, 2) + inner_copies(step):
            copy.wait_recv()
        near_edge = joined(edge_in[step, 0], edge_in[step, 1])
        near_inner = joined(inner_in[step, 0], inner_in[step, 1])
        for place, y in enumerate(BOUNDARY):
            widen(step, fields, y, near_edge, 6 * place)
        for place, y in enumerate(INNER):
            widen(step, fields, y, near_inner, 6 * place)
        for copy in boundary_copies(step)[:4] + y_copies(step):
            copy.wait_recv()
        widen(step, fields, -1, joined(edge_in[step, 2], edge_in[step, 3]), 18)
        widen(step, fields, NY, joined(edge_in[step, 4], edge_in[step, 5]), 0)

    def outer_row(index):
        return index + 4 * (index // 2)

    def inner_row(index):
        return index + 2

    def advance(step, carry):
        arrive(step, (0, 1))
        outer = rows_pass(step, outer_row)
        for copy in y_copies(step + 1):
            copy.start()
        edge_out[step + 1, 0] = pack_rows(step + 1, BOUNDARY)
        for copy in boundary_copies(step + 1):
            copy.start()
        inner = rows_pass(step, inner_row)
        edge_out[step + 1, 1] = pack_rows(step + 1, INNER)
        for copy in inner_copies(step + 1):
            copy.start()
        for place in range(6):
            moments[step * 6 + place] = outer[place] + inner[place]
        return carry

    lax.fori_loop(0, STEPS - 1, advance, 0)

    final = STEPS - 1
    arrive(final, (0,))

    def last_row(y, total):
        old, new = row_force(final, 0, y)
        for c in range(3):
            last[c, y] = new[c]
        return total + dot(old, new)

    moments[19] = lax.fori_loop(0, NY, last_row, jnp.zeros((NZ, NX), F32))
    start_v = [[field[0, 1, c, 2 + y] for c in range(3)] for y in range(NY)]
    moments[18] = sum(dot(value, value) for value in start_v)
    for place in range(20, SLOTS):
        moments[place] = jnp.zeros((NZ, NX), F32)

    wide_lane = lax.broadcasted_iota(jnp.int32, (SLOTS, NX), 1)
    wide_row = lax.broadcasted_iota(jnp.int32, (SLOTS, NX), 0)
    summed = jnp.sum(jnp.sum(moments[...], axis=1), axis=1, keepdims=True)
    flat = jnp.sum(jnp.where(wide_lane == wide_row, summed, 0.0), axis=0, keepdims=True)

    def exchange(value, rows, partners, out, send, recv):
        count = len(partners)
        row_out[out, 0:1] = value
        rows[count : count + 1] = value
        for place, device in enumerate(partners):
            remote(row_out.at[out, 0:1], rows.at[place : place + 1], send, recv, device).start()
        whole = rows.at[0:count]
        pltpu.make_async_copy(whole, whole, recv).wait()
        total = jnp.sum(rows[...], axis=0, keepdims=True)
        pltpu.make_async_copy(whole, whole, send).wait()
        return total

    flat = exchange(flat, row_x, x_partners, 0, rx_send, rx_recv)
    flat = exchange(flat, row_yz, yz_partners, 1, ryz_send, ryz_recv)

    spread = jnp.sum(jnp.where(wide_lane == wide_row, jnp.broadcast_to(flat, (SLOTS, NX)), 0.0), axis=1, keepdims=True)
    spread = jnp.broadcast_to(spread, (SLOTS, NX))
    vv, gg, vg = ([spread[place : place + 1] for place in places] for places in (VV, GG, VG))

    zero = jnp.zeros((1, NX), F32)
    one = jnp.ones((1, NX), F32)
    speed_v, speed_g = [one, zero, zero, zero], [zero] * 4
    pull_v, pull_g = [zero] * 4, [one, zero, zero, zero]
    path_v, path_g = [zero] * 4, [zero] * 4
    for n in range(ITERS):
        terms = range(n if n else 1)

        def quadratic(order):
            total = zero
            for i in terms:
                for j in terms:
                    total = total + speed_v[i] * speed_v[j] * vv[i + j + order]
                    if n:
                        total = total + 2.0 * speed_v[i] * speed_g[j] * vg[i + j + order]
                        total = total + speed_g[i] * speed_g[j] * gg[i + j + order]
            return total

        denominator = quadratic(0)
        numerator = jnp.maximum(-quadratic(1) / FICTIVE_MASS, 0.0)
        damping = 2.0 * jnp.sqrt(numerator / (denominator + 1e-06))
        keep = (2.0 - damping) / (2.0 + damping)
        gain = 2.0 / (FICTIVE_MASS * (2.0 + damping))
        speed_v = [keep * x + gain * y for x, y in zip(speed_v, pull_v)]
        speed_g = [keep * x + gain * y for x, y in zip(speed_g, pull_g)]
        path_v = [x + y for x, y in zip(path_v, speed_v)]
        path_g = [x + y for x, y in zip(path_g, speed_g)]
        pull_v = [pull_v[0]] + [pull_v[j] + speed_v[j - 1] for j in range(1, 4)]
        pull_g = [pull_g[0]] + [pull_g[j] + speed_g[j - 1] for j in range(1, 4)]

    weights = [[jnp.broadcast_to(x, (NZ, NX)) for x in group] for group in (speed_v, speed_g, path_v, path_g)]

    def finish_row(y, carry):
        turned = pl.ds(y, NZ, stride=NY)
        for c in range(3):
            velocities = [field[j, 1, c, 2 + y] for j in range(4)]
            forces = [field[j + 1, 0, c, 2 + y] for j in range(3)] + [last[c, y]]
            v_new = sum(w * x for w, x in zip(weights[0] + weights[1], velocities + forces))
            moved = sum(w * x for w, x in zip(weights[2] + weights[3], velocities + forces))
            v_out[c, turned, :] = v_new
            u_out[c, turned, :] = field[0, 0, c, 2 + y] + moved
        return carry

    lax.fori_loop(0, NY, finish_row, 0)

    for copy in static_y_copies() + static_copies():
        copy.wait_send()

    def drain(step, carry):
        for copy in y_copies(step) + boundary_copies(step) + inner_copies(step):
            copy.wait_send()
        return carry

    lax.fori_loop(0, STEPS, drain, 0)


def shards(displacement, velocity, body_force, modulus, damage_bits):
    rows = NZ * NY
    vmem = pltpu.VMEM
    dma = pltpu.SemaphoreType.DMA
    block = (NZ, NX)
    out = jax.ShapeDtypeStruct((3, rows, NX), F32)
    u, v = pl.pallas_call(
        kernel,
        name="relax",
        out_shape=(out, out),
        in_specs=[pl.BlockSpec(memory_space=pl.ANY)] * 5,
        out_specs=[pl.BlockSpec(memory_space=vmem)] * 2,
        scratch_shapes=[
            vmem((3, rows, NX), F32), vmem((3, rows, NX), F32), vmem((3, rows, NX), F32),
            vmem((rows, NX), F32), vmem((2, rows, NX), jnp.int32),
            vmem((STEPS, 2, 3, NY + 4) + block, F32),
            vmem((3, NY + 4) + block, F32),
            vmem((2, 2, 3, NY + 2) + block, F32),
            vmem((2, 2, 3, NY + 2) + block, F32),
            vmem((2, 2, NY) + block, F32),
            vmem((2, 2, NY) + block, F32),
            vmem((len(FULL), NY) + block, F32),
            vmem(block, F32),
            vmem((3, NY) + block, F32),
            vmem((STEPS, 2) + block, F32),
            vmem((STEPS, 6) + block, F32),
            vmem((STEPS, 2) + block, F32),
            vmem((1, 6) + block, F32),
            vmem((SLOTS,) + block, F32),
            vmem((2, 8, NX), F32),
            vmem((GX, NX), F32),
            vmem((GY * GZ, NX), F32),
            dma((5,)),
            dma((STEPS, 4)), dma((STEPS, 4)),
            dma((STEPS, 6)), dma((STEPS, 6)),
            dma((STEPS, 2)), dma((STEPS, 2)),
            dma((1, 6)), dma((1, 6)),
            dma((4,)), dma((4,)),
            dma, dma, dma, dma,
        ],
        compiler_params=pltpu.CompilerParams(
            collective_id=0, has_side_effects=True, vmem_limit_bytes=32 * 1024 * 1024
        ),
    )(
        displacement.reshape(3, rows, NX),
        velocity.reshape(3, rows, NX),
        body_force.reshape(3, rows, NX),
        modulus.reshape(rows, NX),
        damage_bits.reshape(2, rows, NX),
    )
    return u.reshape(displacement.shape), v.reshape(velocity.shape)


def solution(mesh):
    placed = (
        P(None, None, "gy", "gx"),
        P(None, None, "gy", "gx"),
        P(None, None, "gy", "gx"),
        P(None, "gy", "gx"),
        P(None, None, "gy", "gx"),
    )
    return jax.shard_map(
        shards,
        mesh=mesh,
        in_specs=placed,
        out_specs=(P(None, None, "gy", "gx"), P(None, None, "gy", "gx")),
        check_vma=False,
    )
```

```python
import functools
import math

import jax
import jax.numpy as jnp
from jax import lax
from jax.experimental import pallas as pl
from jax.experimental.pallas import tpu as pltpu
from jax.sharding import PartitionSpec as P

ITERS = 4
STEPS = ITERS
NZ, NY, NX = 8, 8, 128
GX, GY, GZ = 16, 8, 8
MESH = pl.DeviceIdType.MESH
F32 = jnp.float32


def half_offsets():
    result = []
    for step_x in range(-2, 3):
        for step_y in range(-2, 3):
            for step_z in range(-2, 3):
                length_sq = step_x * step_x + step_y * step_y + step_z * step_z
                leading = step_x if step_x != 0 else step_y if step_y != 0 else step_z
                if 0 < length_sq <= 4 and leading > 0:
                    result.append((step_x, step_y, step_z))
    return result


HALF = half_offsets()
FULL = [(entry, number, 1) for number, entry in enumerate(HALF)] + [
    (tuple(-part for part in entry), number, -1) for number, entry in enumerate(HALF)
]
BOND = {entry: place for place, (entry, _, _) in enumerate(FULL)}
FICTIVE_MASS = 2.0 * sum(1.0 / math.sqrt(a * a + b * b + c * c) for a, b, c in HALF)

SIDES = [(-1, 0), (1, 0), (-1, -1), (1, -1), (-1, 1), (1, 1)]


def hops(distance, count):
    return min(distance % count, -distance % count)


X_PARTNERS = sorted(range(1, GX), key=lambda d: -hops(d, GX))
YZ_PARTNERS = sorted(
    [(dy, dz) for dy in range(GY) for dz in range(GZ) if dy or dz],
    key=lambda d: -(hops(d[0], GY) + hops(d[1], GZ)),
)

VV = [18, 0, 1, 6, 7, 12]
GG = [3, 8, 9, 14, 15, 19]
VG = [4, 5, 10, 11, 16, 17]
SLOTS = 24


def kernel(
    u_hbm, v_hbm, body_hbm, mod_hbm, bits_hbm, u_out, v_out,
    raw_u, raw_v, raw_body, raw_mod, raw_bits,
    field, static, ahead, behind, ahead2, behind2, stiff, rims, sides_static, last,
    edge_out, edge_in, inner_in, static_in, moments, row_out, row_x, row_yz,
    load_sem, y_send, y_recv, e_send, e_recv, i_send, i_recv, s_send, s_recv, sy_send, sy_recv,
    rx_send, rx_recv, ryz_send, ryz_recv,
):
    gx, gy = lax.axis_index("gx"), lax.axis_index("gy")
    part_y, part_z = gy // GZ, gy % GZ

    def near(dx, dy):
        return ((gx + dx + GX) % GX, (gy + dy + GY * GZ) % (GY * GZ))

    x_partners = [((gx + d) % GX, gy) for d in X_PARTNERS]
    yz_partners = [
        (gx, ((part_y + dy) % GY) * GZ + (part_z + dz) % GZ) for dy, dz in YZ_PARTNERS
    ]
    near_all = [(dx, dy) for dx in (-1, 0, 1) for dy in (-1, 0, 1) if dx or dy]
    barrier = pltpu.get_barrier_semaphore()
    greeted = [near(dx, dy) for dx, dy in near_all] + x_partners + yz_partners
    for device in greeted:
        pl.semaphore_signal(barrier, inc=1, device_id=device, device_id_type=MESH)

    loads = [
        pltpu.make_async_copy(source, target, load_sem.at[place])
        for place, (source, target) in enumerate(
            [(u_hbm, raw_u), (v_hbm, raw_v), (mod_hbm, raw_mod), (bits_hbm, raw_bits), (body_hbm, raw_body)]
        )
    ]
    for load in loads:
        load.start()

    lane = lax.broadcasted_iota(jnp.int32, (NZ, NX), 1)
    layer = lax.broadcasted_iota(jnp.int32, (NZ, NX), 0)

    def lanes_on(value, amount):
        return pltpu.roll(value, (-amount) % NX, axis=1)

    def layers_on(value, amount):
        return value if amount == 0 else pltpu.roll(value, (-amount) % NZ, axis=0)

    def pack(values):
        total = jnp.zeros((NZ, NX), F32)
        for place, value in enumerate(values):
            total = jnp.where(lane // 4 == place, pltpu.roll(value, (4 * place + 2) % NX, axis=1), total)
        return total

    def joined(left, right):
        return jnp.where(lane % 4 < 2, left, right)

    def rim(both, place):
        return pltpu.roll(both, (2 * NX - 4 * place - 2) % NX, axis=1)

    def plus(value, halo, amount):
        if amount > 0:
            return lanes_on(jnp.where(lane < amount, halo, value), amount)
        return lanes_on(jnp.where(lane >= NX + amount, halo, value), amount)

    def remote(source, target, send, recv, device):
        return pltpu.make_async_remote_copy(
            src_ref=source, dst_ref=target, send_sem=send, recv_sem=recv,
            device_id=device, device_id_type=MESH,
        )

    def y_copies(step):
        return [
            remote(field.at[step, :, :, 9], field.at[step, :, :, 1], y_send.at[step, 0], y_recv.at[step, 0], near(0, 1)),
            remote(field.at[step, :, :, 2], field.at[step, :, :, 10], y_send.at[step, 1], y_recv.at[step, 1], near(0, -1)),
            remote(field.at[step, :, 1, 8], field.at[step, :, 1, 0], y_send.at[step, 2], y_recv.at[step, 2], near(0, 1)),
            remote(field.at[step, :, 1, 3], field.at[step, :, 1, 11], y_send.at[step, 3], y_recv.at[step, 3], near(0, -1)),
        ]

    def static_y_copies():
        return [
            remote(static.at[:, 9], static.at[:, 1], sy_send.at[0], sy_recv.at[0], near(0, 1)),
            remote(static.at[:, 2], static.at[:, 10], sy_send.at[1], sy_recv.at[1], near(0, -1)),
            remote(static.at[0:2, 8], static.at[0:2, 0], sy_send.at[2], sy_recv.at[2], near(0, 1)),
            remote(static.at[0:1, 3], static.at[0:1, 11], sy_send.at[3], sy_recv.at[3], near(0, -1)),
        ]

    def edge_copies(step, source, target, send, recv, count):
        return [
            remote(source, target.at[step, place], send.at[step, place], recv.at[step, place], near(-dx, -dy))
            for place, (dx, dy) in reversed(list(enumerate(SIDES[:count])))
        ]

    def boundary_copies(step):
        return edge_copies(step, edge_out.at[step, 0], edge_in, e_send, e_recv, 6)

    def inner_copies(step):
        return edge_copies(step, edge_out.at[step, 1], inner_in, i_send, i_recv, 2)

    def static_copies():
        return edge_copies(0, sides_static, static_in, s_send, s_recv, 6)

    BOUNDARY = (0, 1, 6, 7)
    INNER = (2, 3, 4, 5)

    def pack_rows(step, rows):
        return pack([field[step, f, c, 2 + y] for y in rows for f in range(2) for c in range(3)])

    for load in loads[:4]:
        load.wait()
    for y in range(NY):
        turned = pl.ds(y, NZ, stride=NY)
        for c in range(3):
            field[0, 0, c, 2 + y] = raw_u[c, turned, :]
            field[0, 1, c, 2 + y] = raw_v[c, turned, :]
        static[0, 2 + y] = raw_mod[turned, :]
        for c in range(2):
            static[1 + c, 2 + y] = raw_bits[c, turned, :].astype(F32)
    edge_out[0, 0] = pack_rows(0, BOUNDARY)
    edge_out[0, 1] = pack_rows(0, INNER)
    sides_static[...] = pack([static[c, 2 + y] for y in range(NY) for c in range(3)])

    pl.semaphore_wait(barrier, len(greeted))
    for copy in static_y_copies() + static_copies() + y_copies(0) + boundary_copies(0) + inner_copies(0):
        copy.start()
    loads[4].wait()

    for copy in static_y_copies() + static_copies():
        copy.wait_recv()
    edge = {-1: joined(static_in[0, 2], static_in[0, 3]), 0: joined(static_in[0, 0], static_in[0, 1]), 1: joined(static_in[0, 4], static_in[0, 5])}
    for y in range(-1, NY + 1):
        side = -1 if y < 0 else 1 if y >= NY else 0
        for c in range(3):
            rims[1, c, 1 + y] = rim(edge[side], 3 * (y - side * NY) + c)
    for y in range(-1, NY + 1):
        for c in range(3):
            value, halo = static[c, 2 + y], rims[1, c, 1 + y]
            if c == 0:
                ahead[1, 0, 0, 1 + y] = plus(value, halo, 1)
            behind[1, 0, c, 1 + y] = plus(value, halo, -1)
            if 0 <= y < NY and c == 0:
                ahead2[1, 0, y] = plus(value, halo, 2)
            if 0 <= y < NY and c != 1:
                behind2[1, c // 2, y] = plus(value, halo, -2)

    column_on = {}
    for a in range(-2, 3):
        on = jnp.logical_and(
            jnp.logical_or(gx > 0, lane + a >= 0), jnp.logical_or(gx < GX - 1, lane + a < NX)
        )
        column_on[a] = on
    layer_on = {c: jnp.logical_and(layer + c >= 0, layer + c < NZ) for c in range(-2, 3)}
    weight = {}
    for a, b, c in BOND:
        if (a, c) not in weight:
            weight[a, c] = jnp.logical_and(column_on[a], layer_on[c]).astype(F32)

    def stiff_row(y, carry):
        def mod_at(a, b):
            if a == 0:
                return static[0, 2 + y + b]
            if abs(a) == 1:
                return (ahead if a > 0 else behind)[1, 0, 0, 1 + y + b]
            return (ahead2 if a > 0 else behind2)[1, 0, y]

        def bits_at(word, a, b):
            if a == 0:
                value = static[1 + word, 2 + y + b]
            elif a == -1:
                value = behind[1, 0, 1 + word, 1 + y + b]
            else:
                value = behind2[1, 1, y]
            return value.astype(jnp.int32)

        row_on = {}
        for b in range(-2, 3):
            on = jnp.logical_and(
                jnp.logical_or(gy > 0, y + b >= 0), jnp.logical_or(gy < GY * GZ - 1, y + b < NY)
            )
            row_on[b] = jnp.where(on, 1.0, 0.0).astype(F32)
        own = static[0, 2 + y]
        words = {}
        partners = {}
        for place, ((a, b, c), number, sign) in enumerate(FULL):
            if (a, b, c) not in partners:
                partners[a, b, c] = layers_on(mod_at(a, b), c)
            length_sq = a * a + b * b + c * c
            scale = 0.5 / (length_sq * math.sqrt(length_sq))
            if length_sq == 4:
                scale = scale * 4.0
            value = (own + partners[a, b, c]) * (weight[a, c] * (row_on[b] * scale))
            where = (number // 8, a, b) if sign < 0 else (number // 8, 0, 0)
            if where not in words:
                words[where] = bits_at(*where)
            broken = jnp.bitwise_and(words[where], 1 << (number % 8))
            if sign < 0:
                broken = layers_on(broken, c)
            stiff[place, y] = jnp.where(broken == 0, value, 0.0)
        return carry

    lax.fori_loop(0, NY, stiff_row, 0)

    def unpack(fields, y, edge_side, place):
        for f in fields:
            for c in range(3):
                rims[f, c, 1 + y] = rim(edge_side, place + 3 * f + c)

    def widen(step, fields, y):
        for f in fields:
            for c in range(3):
                value, halo = field[step, f, c, 2 + y], rims[f, c, 1 + y]
                ahead[0, f, c, 1 + y] = plus(value, halo, 1)
                behind[0, f, c, 1 + y] = plus(value, halo, -1)
                if c == 0 and 0 <= y < NY:
                    ahead2[0, f, y] = plus(value, halo, 2)
                    behind2[0, f, y] = plus(value, halo, -2)

    def row_force(step, f, y):
        own = [field[step, f, c, 2 + y] for c in range(3)]
        force = [jnp.zeros((NZ, NX), F32) for _ in range(3)]

        def bond(a, b, c):
            return stiff[BOND[a, b, c], y]

        for c in (-1, 1, -2, 2):
            force[2] += bond(0, 0, c) * (layers_on(own[2], c) - own[2])
        for b in (-1, 1):
            pair = [None if c == 0 else field[step, f, c, 2 + y + b] for c in range(3)]
            pulls = {}
            for gamma in (-1, 0, 1):
                c = gamma * b
                partner = pair[1] + gamma * pair[2] if gamma else pair[1]
                mine = own[1] + gamma * own[2] if gamma else own[1]
                pulls[gamma] = bond(0, b, c) * (layers_on(partner, c) - mine)
            force[1] += pulls[-1] + pulls[0] + pulls[1]
            force[2] += pulls[1] - pulls[-1]
        for b in (-2, 2):
            force[1] += bond(0, b, 0) * (field[step, f, 1, 2 + y + b] - own[1])
        force[0] += bond(2, 0, 0) * (ahead2[0, f, y] - own[0])
        force[0] += bond(-2, 0, 0) * (behind2[0, f, y] - own[0])
        for beta in (-1, 0, 1):
            mine = own[0] + beta * own[1] if beta else own[0]
            for a in (-1, 1):
                b = a * beta
                source = ahead if a > 0 else behind
                pair = [source[0, f, c, 1 + y + b] for c in range(3)]
                partner = pair[0] + beta * pair[1] if beta else pair[0]
                pulls = {}
                for gamma in (-1, 0, 1):
                    c = gamma * a
                    there = partner + gamma * pair[2] if gamma else partner
                    here = mine + gamma * own[2] if gamma else mine
                    pulls[gamma] = bond(a, b, c) * (layers_on(there, c) - here)
                total = pulls[-1] + pulls[0] + pulls[1]
                force[0] += total
                if beta:
                    force[1] += beta * total
                force[2] += pulls[1] - pulls[-1]
        return own, force

    def dot(first, second):
        return first[0] * second[0] + first[1] * second[1] + first[2] * second[2]

    def rows_pass(step, first_row):
        def row(index, sums):
            y = first_row(index)
            old_g, new_g = row_force(step, 0, y)
            if step == 0:
                new_g = [new_g[c] + raw_body[c, pl.ds(y, NZ, stride=NY), :] for c in range(3)]
            old_v, new_v = row_force(step, 1, y)
            for c in range(3):
                field[step + 1, 0, c, 2 + y] = new_g[c]
                field[step + 1, 1, c, 2 + y] = new_v[c]
            terms = [
                dot(old_v, new_v), dot(new_v, new_v), dot(old_g, new_g),
                dot(new_g, new_g), dot(old_v, new_g), dot(new_v, new_g),
            ]
            return tuple(total + term for total, term in zip(sums, terms))

        sums = lax.fori_loop(0, 4, row, (jnp.zeros((NZ, NX), F32),) * 6)
        return sums

    def arrive(step, fields):
        for copy in edge_copies(step, edge_out.at[step, 0], edge_in, e_send, e_recv, 2) + inner_copies(step):
            copy.wait_recv()
        near_edge = joined(edge_in[step, 0], edge_in[step, 1])
        near_inner = joined(inner_in[step, 0], inner_in[step, 1])
        for place, y in enumerate(BOUNDARY):
            unpack(fields, y, near_edge, 6 * place)
        for place, y in enumerate(INNER):
            unpack(fields, y, near_inner, 6 * place)
        for y in range(NY):
            widen(step, fields, y)
        for copy in boundary_copies(step)[:4] + y_copies(step):
            copy.wait_recv()
        unpack(fields, -1, joined(edge_in[step, 2], edge_in[step, 3]), 18)
        unpack(fields, NY, joined(edge_in[step, 4], edge_in[step, 5]), 0)
        widen(step, fields, -1)
        widen(step, fields, NY)

    def outer_row(index):
        return index + 4 * (index // 2)

    def inner_row(index):
        return index + 2

    def advance(step):
        arrive(step, (0, 1))
        outer = rows_pass(step, outer_row)
        for copy in y_copies(step + 1):
            copy.start()
        edge_out[step + 1, 0] = pack_rows(step + 1, BOUNDARY)
        for copy in boundary_copies(step + 1):
            copy.start()
        inner = rows_pass(step, inner_row)
        edge_out[step + 1, 1] = pack_rows(step + 1, INNER)
        for copy in inner_copies(step + 1):
            copy.start()
        for place in range(6):
            moments[step * 6 + place] = outer[place] + inner[place]

    for step in range(STEPS - 1):
        advance(step)

    final = STEPS - 1
    arrive(final, (0,))

    def last_row(y, total):
        old, new = row_force(final, 0, y)
        for c in range(3):
            last[c, y] = new[c]
        return total + dot(old, new)

    moments[19] = lax.fori_loop(0, NY, last_row, jnp.zeros((NZ, NX), F32))
    start_v = [[field[0, 1, c, 2 + y] for c in range(3)] for y in range(NY)]
    moments[18] = sum(dot(value, value) for value in start_v)
    for place in range(20, SLOTS):
        moments[place] = jnp.zeros((NZ, NX), F32)

    wide_lane = lax.broadcasted_iota(jnp.int32, (SLOTS, NX), 1)
    wide_row = lax.broadcasted_iota(jnp.int32, (SLOTS, NX), 0)
    summed = jnp.sum(jnp.sum(moments[...], axis=1), axis=1, keepdims=True)
    flat = jnp.sum(jnp.where(wide_lane == wide_row, summed, 0.0), axis=0, keepdims=True)

    def exchange(value, rows, partners, out, send, recv):
        count = len(partners)
        row_out[out, 0:1] = value
        rows[count : count + 1] = value
        for place, device in enumerate(partners):
            remote(row_out.at[out, 0:1], rows.at[place : place + 1], send, recv, device).start()
        whole = rows.at[0:count]
        pltpu.make_async_copy(whole, whole, recv).wait()
        total = jnp.sum(rows[...], axis=0, keepdims=True)
        pltpu.make_async_copy(whole, whole, send).wait()
        return total

    flat = exchange(flat, row_x, x_partners, 0, rx_send, rx_recv)
    flat = exchange(flat, row_yz, yz_partners, 1, ryz_send, ryz_recv)

    spread = jnp.sum(jnp.where(wide_lane == wide_row, jnp.broadcast_to(flat, (SLOTS, NX)), 0.0), axis=1, keepdims=True)
    spread = jnp.broadcast_to(spread, (SLOTS, NX))
    vv, gg, vg = ([spread[place : place + 1] for place in places] for places in (VV, GG, VG))

    zero = jnp.zeros((1, NX), F32)
    one = jnp.ones((1, NX), F32)
    speed_v, speed_g = [one, zero, zero, zero], [zero] * 4
    pull_v, pull_g = [zero] * 4, [one, zero, zero, zero]
    path_v, path_g = [zero] * 4, [zero] * 4
    for n in range(ITERS):
        terms = range(n if n else 1)

        def quadratic(order):
            total = zero
            for i in terms:
                for j in terms:
                    total = total + speed_v[i] * speed_v[j] * vv[i + j + order]
                    if n:
                        total = total + 2.0 * speed_v[i] * speed_g[j] * vg[i + j + order]
                        total = total + speed_g[i] * speed_g[j] * gg[i + j + order]
            return total

        denominator = quadratic(0)
        numerator = jnp.maximum(-quadratic(1) / FICTIVE_MASS, 0.0)
        damping = 2.0 * jnp.sqrt(numerator / (denominator + 1e-06))
        keep = (2.0 - damping) / (2.0 + damping)
        gain = 2.0 / (FICTIVE_MASS * (2.0 + damping))
        speed_v = [keep * x + gain * y for x, y in zip(speed_v, pull_v)]
        speed_g = [keep * x + gain * y for x, y in zip(speed_g, pull_g)]
        path_v = [x + y for x, y in zip(path_v, speed_v)]
        path_g = [x + y for x, y in zip(path_g, speed_g)]
        pull_v = [pull_v[0]] + [pull_v[j] + speed_v[j - 1] for j in range(1, 4)]
        pull_g = [pull_g[0]] + [pull_g[j] + speed_g[j - 1] for j in range(1, 4)]

    weights = [[jnp.broadcast_to(x, (NZ, NX)) for x in group] for group in (speed_v, speed_g, path_v, path_g)]

    def finish_row(y, carry):
        turned = pl.ds(y, NZ, stride=NY)
        for c in range(3):
            velocities = [field[j, 1, c, 2 + y] for j in range(4)]
            forces = [field[j + 1, 0, c, 2 + y] for j in range(3)] + [last[c, y]]
            v_new = sum(w * x for w, x in zip(weights[0] + weights[1], velocities + forces))
            moved = sum(w * x for w, x in zip(weights[2] + weights[3], velocities + forces))
            v_out[c, turned, :] = v_new
            u_out[c, turned, :] = field[0, 0, c, 2 + y] + moved
        return carry

    lax.fori_loop(0, NY, finish_row, 0)

    for copy in static_y_copies() + static_copies():
        copy.wait_send()

    def drain(step, carry):
        for copy in y_copies(step) + boundary_copies(step) + inner_copies(step):
            copy.wait_send()
        return carry

    lax.fori_loop(0, STEPS, drain, 0)


def shards(displacement, velocity, body_force, modulus, damage_bits):
    rows = NZ * NY
    vmem = pltpu.VMEM
    dma = pltpu.SemaphoreType.DMA
    block = (NZ, NX)
    out = jax.ShapeDtypeStruct((3, rows, NX), F32)
    u, v = pl.pallas_call(
        kernel,
        name="relax",
        out_shape=(out, out),
        in_specs=[pl.BlockSpec(memory_space=pl.ANY)] * 5,
        out_specs=[pl.BlockSpec(memory_space=vmem)] * 2,
        scratch_shapes=[
            vmem((3, rows, NX), F32), vmem((3, rows, NX), F32), vmem((3, rows, NX), F32),
            vmem((rows, NX), F32), vmem((2, rows, NX), jnp.int32),
            vmem((STEPS, 2, 3, NY + 4) + block, F32),
            vmem((3, NY + 4) + block, F32),
            vmem((2, 2, 3, NY + 2) + block, F32),
            vmem((2, 2, 3, NY + 2) + block, F32),
            vmem((2, 2, NY) + block, F32),
            vmem((2, 2, NY) + block, F32),
            vmem((len(FULL), NY) + block, F32),
            vmem((2, 3, NY + 2) + block, F32),
            vmem(block, F32),
            vmem((3, NY) + block, F32),
            vmem((STEPS, 2) + block, F32),
            vmem((STEPS, 6) + block, F32),
            vmem((STEPS, 2) + block, F32),
            vmem((1, 6) + block, F32),
            vmem((SLOTS,) + block, F32),
            vmem((2, 8, NX), F32),
            vmem((GX, NX), F32),
            vmem((GY * GZ, NX), F32),
            dma((5,)),
            dma((STEPS, 4)), dma((STEPS, 4)),
            dma((STEPS, 6)), dma((STEPS, 6)),
            dma((STEPS, 2)), dma((STEPS, 2)),
            dma((1, 6)), dma((1, 6)),
            dma((4,)), dma((4,)),
            dma, dma, dma, dma,
        ],
        compiler_params=pltpu.CompilerParams(
            collective_id=0, has_side_effects=True, vmem_limit_bytes=60 * 1024 * 1024
        ),
    )(
        displacement.reshape(3, rows, NX),
        velocity.reshape(3, rows, NX),
        body_force.reshape(3, rows, NX),
        modulus.reshape(rows, NX),
        damage_bits.reshape(2, rows, NX),
    )
    return u.reshape(displacement.shape), v.reshape(velocity.shape)


def solution(mesh):
    placed = (
        P(None, None, "gy", "gx"),
        P(None, None, "gy", "gx"),
        P(None, None, "gy", "gx"),
        P(None, "gy", "gx"),
        P(None, None, "gy", "gx"),
    )
    return jax.shard_map(
        shards,
        mesh=mesh,
        in_specs=placed,
        out_specs=(P(None, None, "gy", "gx"), P(None, None, "gy", "gx")),
        check_vma=False,
    )
```

```python
import functools
import math

import jax
import jax.numpy as jnp
from jax import lax
from jax.experimental import pallas as pl
from jax.experimental.pallas import tpu as pltpu
from jax.sharding import PartitionSpec as P

ITERS = 4
NZ, NY, NX = 8, 8, 128
GX, GY, GZ = 16, 8, 8
MESH = pl.DeviceIdType.MESH
F32 = jnp.float32


def half_offsets():
    result = []
    for step_x in range(-2, 3):
        for step_y in range(-2, 3):
            for step_z in range(-2, 3):
                length_sq = step_x * step_x + step_y * step_y + step_z * step_z
                leading = step_x if step_x != 0 else step_y if step_y != 0 else step_z
                if 0 < length_sq <= 4 and leading > 0:
                    result.append((step_x, step_y, step_z))
    return result


HALF = half_offsets()
FULL = [(entry, number, 1) for number, entry in enumerate(HALF)] + [
    (tuple(-part for part in entry), number, -1) for number, entry in enumerate(HALF)
]
BOND = {entry: place for place, (entry, _, _) in enumerate(FULL)}
FICTIVE_MASS = 2.0 * sum(1.0 / math.sqrt(a * a + b * b + c * c) for a, b, c in HALF)

SIDES = [(-1, 0), (1, 0), (-1, -1), (1, -1), (-1, 1), (1, 1)]


def hops(distance, count):
    return min(distance % count, -distance % count)


CHIPS = GX // 2
X_STEPS = sorted(range(CHIPS), key=lambda d: -hops(d, CHIPS))
YZ_STEPS = sorted(
    [(dy, dz) for dy in range(GY) for dz in range(GZ) if dy or dz],
    key=lambda d: -(hops(d[0], GY) + hops(d[1], GZ)),
)

U, V0, G0, V1, G1, V2, G2, V3, G3 = range(9)
CHAIN_V, CHAIN_G = (V0, V1, V2, V3), (G0, G1, G2, G3)
EARLY = [(V0, V0), (V0, V1), (V1, V1), (G0, G0), (G0, G1), (G1, G1), (V0, G0), (V1, G0), (V1, G1)]
MIDDLE = [(V1, V2), (V2, V2), (V2, V3), (V2, G1)]
LATE = [(G1, G2), (G2, G2), (V2, G2), (V3, G2), (G2, G3)]
PAIRS = EARLY + MIDDLE + LATE
SLOTS = 24


def moment_slots(first, second):
    return [
        PAIRS.index(next((first[i], second[k - i]) for i in range(4) if 0 <= k - i < 4 and (first[i], second[k - i]) in PAIRS))
        for k in range(6)
    ]


VV, GG, VG = moment_slots(CHAIN_V, CHAIN_V), moment_slots(CHAIN_G, CHAIN_G), moment_slots(CHAIN_V, CHAIN_G)
REACH = 4
ROWS = NY + 2 * REACH
INNER = (2, 3, 4, 5)
OUTER = (-2, -1, 0, 1, 6, 7, 8, 9)


def kernel(
    u_hbm, v_hbm, body_hbm, mod_hbm, bits_hbm, result,
    raw_u, raw_v, raw_body, raw_mod, raw_bits,
    field, static, force, near_x, far_x, stiff, weights, edge_out, edge_in, moments, row_out, row_x, row_yz,
    load_sem, y_send, y_recv, side_send, side_recv, rx_send, rx_recv, ryz_send, ryz_recv, known,
):
    gx, gy = lax.axis_index("gx"), lax.axis_index("gy")
    part_y, part_z, core = gy // GZ, gy % GZ, gx % 2

    def near(dx, dy):
        return ((gx + dx + GX) % GX, (gy + dy + GY * GZ) % (GY * GZ))

    def across(dy, dz):
        return ((part_y + dy) % GY) * GZ + (part_z + dz) % GZ

    greeted = [near(dx, dy) for dx in (-1, 0, 1) for dy in (-1, 0, 1) if dx or dy]
    x_partners = [((gx + d) % GX, gy) for d in sorted(range(1, GX), key=lambda d: -hops(d, GX))]
    yz_partners = [(gx, across(dy, dz)) for dy, dz in YZ_STEPS]
    greeted += [near(dx, 0) for dx in (-2, 2)]
    boxes = [(dy, dz) for dy in (-1, 0, 1) for dz in (-1, 0, 1) if dy or dz]
    greeted += [(gx, across(dy, dz)) for dy, dz in boxes]
    rounds = [
        [near(dx * k, 0) for dx in (-2, 2)] + [(gx, across(dy * k, dz * k)) for dy, dz in boxes]
        for k in (1, 2)
    ]

    def call(number):
        for device in rounds[number]:
            pl.semaphore_signal(known.at[number], inc=1, device_id=device, device_id_type=MESH)

    def heard(number):
        pl.semaphore_wait(known.at[number], len(rounds[number]))

    barrier = pltpu.get_barrier_semaphore()

    def greet(devices):
        for device in devices:
            pl.semaphore_signal(barrier, inc=1, device_id=device, device_id_type=MESH)

    greet(greeted)
    loads = [
        pltpu.make_async_copy(source, target, load_sem.at[place])
        for place, (source, target) in enumerate(
            [(u_hbm, raw_u), (mod_hbm, raw_mod), (bits_hbm, raw_bits), (v_hbm, raw_v), (body_hbm, raw_body)]
        )
    ]
    for load in loads:
        load.start()

    lane = lax.broadcasted_iota(jnp.int32, (NZ, NX), 1)
    layer = lax.broadcasted_iota(jnp.int32, (NZ, NX), 0)
    nothing = jnp.zeros((NZ, NX), F32)

    def lanes_on(value, amount):
        return pltpu.roll(value, (-amount) % NX, axis=1)

    def layers_on(value, amount):
        return value if amount == 0 else pltpu.roll(value, (-amount) % NZ, axis=0)

    def plus(value, other, amount):
        if amount > 0:
            return lanes_on(jnp.where(lane < amount, other, value), amount)
        return lanes_on(jnp.where(lane >= NX + amount, other, value), amount)

    def pack(values, width, start=0):
        total = nothing
        for place, value in enumerate(values):
            turned = pltpu.roll(value, (8 * place + start + width) % NX, axis=1)
            total = jnp.where(lane // 8 == place, turned, total)
        return total

    def remote(source, target, send, recv, device):
        return pltpu.make_async_remote_copy(
            src_ref=source, dst_ref=target, send_sem=send, recv_sem=recv,
            device_id=device, device_id_type=MESH,
        )

    def row_copies(number):
        ref, deep, up, down = [
            (static.at[0], 4, slice(0, 2), slice(0, 1)),
            (field.at[U, 0], 4, slice(1, 2), slice(1, 2)),
            (field.at[V0, 0], 2, slice(1, 2), slice(1, 2)),
            (force.at[0], 2, slice(1, 2), slice(1, 2)),
            (field.at[V1, 0], 4, slice(1, 2), slice(1, 2)),
            (field.at[G1, 0], 4, slice(1, 2), slice(1, 2)),
        ][number]
        top, low = REACH + NY, REACH
        spans = [
            (slice(0, 3), slice(top - deep + 1, top), slice(low - deep + 1, low), 1),
            (slice(0, 3), slice(low, low + deep - 1), slice(top, top + deep - 1), -1),
            (up, slice(top - deep, top - deep + 1), slice(low - deep, low - deep + 1), 1),
            (down, slice(low + deep - 1, low + deep), slice(top + deep - 1, top + deep), -1),
        ]
        return [
            remote(ref.at[what, source], ref.at[what, target], y_send.at[number, place], y_recv.at[number, place], near(0, way))
            for place, (what, source, target, way) in enumerate(spans)
        ]

    def side_copies(group):
        first, last = [(0, 3), (3, 4), (4, 5)][group]
        copies = []
        for place, (dx, dy) in enumerate(SIDES):
            half = slice(0, 2) if dy == 0 else slice(1, 2) if dy < 0 else slice(0, 1)
            copies.append(
                remote(
                    edge_out.at[first:last, half], edge_in.at[first:last, place, half],
                    side_send.at[group, place], side_recv.at[group, place], near(-dx, -dy),
                )
            )
        return copies

    for load in loads:
        load.wait()
    for y in range(NY):
        turned = pl.ds(y, NZ, stride=NY)
        for c in range(3):
            field[U, 0, c, REACH + y] = raw_u[c, turned, :]
            field[V0, 0, c, REACH + y] = raw_v[c, turned, :]
            force[0, c, REACH + y] = raw_body[c, turned, :]
        static[0, 0, REACH + y] = raw_mod[turned, :]
        for c in range(2):
            static[0, 1 + c, REACH + y] = raw_bits[c, turned, :].astype(F32)

    def rows_of(ref, half):
        return [ref[c, REACH + 4 * half + y] for y in range(4) for c in range(3)]

    for half in range(2):
        edge_out[0, half] = pack(rows_of(static.at[0], half), 4)
        edge_out[1, half] = pack(rows_of(field.at[U, 0], half), 4)
        edge_out[2, half] = jnp.where(
            lane % 8 < 4, pack(rows_of(field.at[V0, 0], half), 2), pack(rows_of(force.at[0], half), 2, 4)
        )

    pl.semaphore_wait(barrier, len(greeted))
    for number in range(4):
        for copy in row_copies(number):
            copy.start()
        if number == 0:
            for copy in side_copies(0):
                copy.start()
    call(0)
    heard(0)
    call(1)

    def unpack(ref, number, half, sides, first, width, start=0, depth=4):
        both = jnp.where(
            lane % (2 * width) < width, edge_in[number, sides, half], edge_in[number, sides + 1, half]
        )
        for y in range(4):
            if first < 0 and y < 4 - depth or first >= NY and y >= depth:
                continue
            for c in range(3):
                slot = 8 * (3 * y + c) + start + width
                ref[c, REACH + first + y] = pltpu.roll(both, (2 * NX - slot) % NX, axis=1)

    def shift(value_ref, slot, rows, far_rows, kinds=(0, 1), comps=(0, 1, 2), ahead=(0, 1, 2), far=((0, 0, 0), (1, 0, 0))):
        for y in rows:
            row = REACH + y
            for e in kinds:
                for c in comps:
                    value, other = value_ref[e, c, row], value_ref[1 - e, c, row]
                    if c in ahead:
                        near_x[slot, e, 0, c, row] = plus(value, other, 1)
                    near_x[slot, e, 1, c, row] = plus(value, other, -1)
                    for way, which, place in far:
                        if which == c and y in far_rows:
                            far_x[slot, e, way, place, row] = plus(value, other, 2 - 4 * way)

    columns = {0: lane, 1: jnp.where(lane < NX // 2, lane + NX, lane - NX)}
    for e in range(2):
        for a in range(-2, 3):
            there = columns[e] + a
            on = jnp.logical_and(jnp.logical_or(gx > 0, there >= 0), jnp.logical_or(gx < GX - 1, there < NX))
            for c in range(-2, 3):
                if a * a + c * c <= 4:
                    inside = jnp.logical_and(layer + c >= 0, layer + c < NZ)
                    weights[e, 5 * (a + 2) + c + 2] = jnp.logical_and(on, inside).astype(F32)

    def stiff_row(y):
        row_on = {}
        for b in range(-2, 3):
            on = jnp.logical_and(
                jnp.logical_or(gy > 0, y + b >= 0), jnp.logical_or(gy < GY * GZ - 1, y + b < NY)
            )
            row_on[b] = jnp.where(on, 1.0, 0.0).astype(F32)
        for e in range(2):

            def at(c, a, b):
                row = REACH + y + b
                if a == 0:
                    return static[e, c, row]
                if abs(a) == 1:
                    return near_x[0, e, 0 if a > 0 else 1, c, row]
                return far_x[0, e, 0 if a > 0 else 1, 0 if c == 0 else 1, row]

            own = static[e, 0, REACH + y]
            words, partners, values = {}, {}, []
            for (a, b, c), number, sign in FULL:
                if (a, b, c) not in partners:
                    partners[a, b, c] = layers_on(at(0, a, b), c)
                length_sq = a * a + b * b + c * c
                scale = 0.5 / (length_sq * math.sqrt(length_sq)) * (4.0 if length_sq == 4 else 1.0)
                value = (own + partners[a, b, c]) * (weights[e, 5 * (a + 2) + c + 2] * (row_on[b] * scale))
                where = (number // 8, a, b) if sign < 0 else (number // 8, 0, 0)
                if where not in words:
                    words[where] = at(1 + where[0], where[1], where[2]).astype(jnp.int32)
                broken = jnp.bitwise_and(words[where], 1 << (number % 8))
                if sign < 0:
                    broken = layers_on(broken, c)
                values.append(jnp.where(broken == 0, value, 0.0))
            for place, value in enumerate(values):
                stiff[e, place, 2 + y] = value

    def pull(f, slot, e, y):
        row = REACH + y
        own = [field[f, e, c, row] for c in range(3)]
        total = [nothing, nothing, nothing]

        def bond(a, b, c):
            return stiff[e, BOND[a, b, c], 2 + y]

        for c in (-1, 1, -2, 2):
            total[2] += bond(0, 0, c) * (layers_on(own[2], c) - own[2])
        for b in (-1, 1):
            pair = [None if c == 0 else field[f, e, c, row + b] for c in range(3)]
            pulls = {}
            for gamma in (-1, 0, 1):
                c = gamma * b
                partner = pair[1] + gamma * pair[2] if gamma else pair[1]
                mine = own[1] + gamma * own[2] if gamma else own[1]
                pulls[gamma] = bond(0, b, c) * (layers_on(partner, c) - mine)
            total[1] += pulls[-1] + pulls[0] + pulls[1]
            total[2] += pulls[1] - pulls[-1]
        for b in (-2, 2):
            total[1] += bond(0, b, 0) * (field[f, e, 1, row + b] - own[1])
        for way in range(2):
            total[0] += bond(2 - 4 * way, 0, 0) * (far_x[slot, e, way, 0, row] - own[0])
        for beta in (-1, 0, 1):
            mine = own[0] + beta * own[1] if beta else own[0]
            for way, a in enumerate((1, -1)):
                b = a * beta
                pair = [near_x[slot, e, way, c, row + b] for c in range(3)]
                partner = pair[0] + beta * pair[1] if beta else pair[0]
                pulls = {}
                for gamma in (-1, 0, 1):
                    c = gamma * a
                    there = partner + gamma * pair[2] if gamma else partner
                    here = mine + gamma * own[2] if gamma else mine
                    pulls[gamma] = bond(a, b, c) * (layers_on(there, c) - here)
                both = pulls[-1] + pulls[0] + pulls[1]
                total[0] += both
                if beta:
                    total[1] += beta * both
                total[2] += pulls[1] - pulls[-1]
        return total

    def advance(f, slot, to, kinds, y):
        row = REACH + y
        news = [pull(f, slot, e, y) for e in kinds]
        if to == G0:
            news = [[new[c] + force[e, c, row] for c in range(3)] for e, new in zip(kinds, news)]
        for e, new in zip(kinds, news):
            for c in range(3):
                field[to, e, c, row] = new[c]

    def loop(count, where, *work):
        def one(index, carry):
            y = where(index)
            for step in work:
                step(y)
            return carry

        lax.fori_loop(0, count, one, 0)

    def inner(index):
        return index + 2

    def outer(index):
        return index - 2 + 4 * (index // 4)

    def rim(index):
        return index + 4 * (index // 2)

    def all_rows(index):
        return index

    def dot(first, second):
        return first[0] * second[0] + first[1] * second[1] + first[2] * second[2]

    def gather(pairs, last_step=None):
        used = sorted({f for pair in pairs for f in pair})

        def row(y, sums):
            if last_step is not None:
                last_step(y)
            have = {f: [field[f, 0, c, REACH + y] for c in range(3)] for f in used}
            return tuple(total + dot(have[a], have[b]) for total, (a, b) in zip(sums, pairs))

        sums = lax.fori_loop(0, NY, row, (nothing,) * len(pairs))
        for pair, total in zip(pairs, sums):
            moments[PAIRS.index(pair)] = total

    own_rows, outside = list(range(NY)), [-3, -2, -1, 8, 9, 10]
    wide_rows = set(range(-2, NY + 2))

    def halves(ref, number, width, start=0, depth=4, sides=(0,)):
        if 0 in sides:
            unpack(ref, number, 0, 0, 0, width, start)
            unpack(ref, number, 1, 0, 4, width, start)
        else:
            unpack(ref, number, 1, 2, -4, width, start, depth)
            unpack(ref, number, 0, 4, NY, width, start, depth)

    def shift_static(rows):
        shift(static, 0, rows, wide_rows, ahead=(0,), far=((0, 0, 0), (1, 0, 0), (1, 2, 1)))

    for copy in side_copies(0)[:2]:
        copy.wait_recv()
    halves(static.at[1], 0, 4)
    halves(field.at[U, 1], 1, 4)
    halves(field.at[V0, 1], 2, 2)
    halves(force.at[1], 2, 2, 4)
    shift_static(own_rows)
    shift(field.at[U], 1, own_rows, wide_rows)
    shift(field.at[V0], 2, own_rows, set(own_rows), kinds=(0,))
    loop(4, inner, stiff_row)
    loop(4, inner, lambda y: advance(V0, 2, V1, (0,), y), lambda y: advance(U, 1, G0, (0, 1), y))
    heard(1)
    for copy in side_copies(0)[2:] + row_copies(0) + row_copies(1) + row_copies(2) + row_copies(3):
        copy.wait_recv()
    halves(static.at[1], 0, 4, sides=(1,))
    halves(field.at[U, 1], 1, 4, sides=(1,))
    halves(field.at[V0, 1], 2, 2, depth=1, sides=(1,))
    halves(force.at[1], 2, 2, 4, depth=2, sides=(1,))
    shift_static(outside)
    shift(field.at[V0], 2, [-1, 8], set(), kinds=(0,))
    shift(field.at[U], 1, outside, wide_rows)
    loop(8, outer, stiff_row)
    loop(4, rim, lambda y: advance(V0, 2, V1, (0,), y))
    for copy in row_copies(4):
        copy.start()
    for half in range(2):
        edge_out[3, half] = pack(rows_of(field.at[V1, 0], half), 4)
    for copy in side_copies(1):
        copy.start()
    loop(8, outer, lambda y: advance(U, 1, G0, (0, 1), y))
    shift(field.at[G0], 3, [-1] + own_rows + [8], set(own_rows), kinds=(0,))
    loop(4, rim, lambda y: advance(G0, 3, G1, (0,), y))
    loop(4, inner, lambda y: advance(G0, 3, G1, (0,), y))
    for copy in row_copies(5):
        copy.start()
    for half in range(2):
        edge_out[4, half] = pack(rows_of(field.at[G1, 0], half), 4)
    for copy in side_copies(2):
        copy.start()

    gather(EARLY)
    for copy in side_copies(1) + row_copies(4):
        copy.wait_recv()
    for side in range(2):
        halves(field.at[V1, 1], 3, 4, sides=(side,))
    shift(field.at[V1], 4, own_rows + outside, wide_rows)
    loop(12, lambda index: index - 2, lambda y: advance(V1, 4, V2, (0, 1), y))
    shift(field.at[V2], 5, [-1] + own_rows + [8], set(own_rows), kinds=(0,))
    gather(MIDDLE, lambda y: advance(V2, 5, V3, (0,), y))
    for copy in side_copies(2)[:2]:
        copy.wait_recv()
    halves(field.at[G1, 1], 4, 4)
    shift(field.at[G1], 6, own_rows, wide_rows)
    loop(4, inner, lambda y: advance(G1, 6, G2, (0, 1), y))
    for copy in side_copies(2)[2:] + row_copies(5):
        copy.wait_recv()
    halves(field.at[G1, 1], 4, 4, sides=(1,))
    shift(field.at[G1], 6, outside, wide_rows)
    loop(8, outer, lambda y: advance(G1, 6, G2, (0, 1), y))
    shift(field.at[G2], 7, [-1] + own_rows + [8], set(own_rows), kinds=(0,))
    for place in range(len(PAIRS), SLOTS):
        moments[place] = nothing
    gather(LATE, lambda y: advance(G2, 7, G3, (0,), y))

    wide_lane = lax.broadcasted_iota(jnp.int32, (SLOTS, NX), 1)
    wide_row = lax.broadcasted_iota(jnp.int32, (SLOTS, NX), 0)
    summed = jnp.sum(jnp.sum(moments[...], axis=1), axis=1, keepdims=True)
    flat = jnp.sum(jnp.where(wide_lane == wide_row, summed, 0.0), axis=0, keepdims=True)

    def exchange(value, rows, partners, out, send, recv):
        count = len(partners)
        row_out[out, 0:1] = value
        rows[count : count + 1] = value
        for place, device in enumerate(partners):
            remote(row_out.at[out, 0:1], rows.at[place : place + 1], send, recv, device).start()
        whole = rows.at[0:count]
        pltpu.make_async_copy(whole, whole, recv).wait()
        return jnp.sum(rows[...], axis=0, keepdims=True)

    flat = exchange(flat, row_x, x_partners, 0, rx_send, rx_recv)
    flat = exchange(flat, row_yz, yz_partners, 1, ryz_send, ryz_recv)

    spread = jnp.sum(jnp.where(wide_lane == wide_row, jnp.broadcast_to(flat, (SLOTS, NX)), 0.0), axis=1, keepdims=True)
    spread = jnp.broadcast_to(spread, (SLOTS, NX))
    vv, gg, vg = ([spread[place : place + 1] for place in places] for places in (VV, GG, VG))

    zero = jnp.zeros((1, NX), F32)
    one = jnp.ones((1, NX), F32)
    speed_v, speed_g = [one, zero, zero, zero], [zero] * 4
    pull_v, pull_g = [zero] * 4, [one, zero, zero, zero]
    path_v, path_g = [zero] * 4, [zero] * 4
    for n in range(ITERS):
        terms = range(n if n else 1)

        def quadratic(order):
            total = zero
            for i in terms:
                for j in terms:
                    total = total + speed_v[i] * speed_v[j] * vv[i + j + order]
                    if n:
                        total = total + 2.0 * speed_v[i] * speed_g[j] * vg[i + j + order]
                        total = total + speed_g[i] * speed_g[j] * gg[i + j + order]
            return total

        denominator = quadratic(0)
        numerator = jnp.maximum(-quadratic(1) / FICTIVE_MASS, 0.0)
        damping = 2.0 * jnp.sqrt(numerator / (denominator + 1e-06))
        keep = (2.0 - damping) / (2.0 + damping)
        gain = 2.0 / (FICTIVE_MASS * (2.0 + damping))
        speed_v = [keep * x + gain * y for x, y in zip(speed_v, pull_v)]
        speed_g = [keep * x + gain * y for x, y in zip(speed_g, pull_g)]
        path_v = [x + y for x, y in zip(path_v, speed_v)]
        path_g = [x + y for x, y in zip(path_g, speed_g)]
        pull_v = [pull_v[0]] + [pull_v[j] + speed_v[j - 1] for j in range(1, 4)]
        pull_g = [pull_g[0]] + [pull_g[j] + speed_g[j - 1] for j in range(1, 4)]

    factors = [[jnp.broadcast_to(x, (NZ, NX)) for x in group] for group in (speed_v, speed_g, path_v, path_g)]

    def finish_row(y, carry):
        turned, row = pl.ds(y, NZ, stride=NY), REACH + y
        for c in range(3):
            basis = [field[f, 0, c, row] for f in CHAIN_V + CHAIN_G]
            result[1, c, turned, :] = sum(w * x for w, x in zip(factors[0] + factors[1], basis))
            moved = sum(w * x for w, x in zip(factors[2] + factors[3], basis))
            result[0, c, turned, :] = field[U, 0, c, row] + moved
        return carry

    lax.fori_loop(0, NY, finish_row, 0)
    for number in range(6):
        for copy in row_copies(number):
            copy.wait_send()
    for group in range(3):
        for copy in side_copies(group):
            copy.wait_send()

    for rows, count, sem in ((row_x, len(x_partners), rx_send), (row_yz, len(yz_partners), ryz_send)):
        whole = rows.at[0:count]
        pltpu.make_async_copy(whole, whole, sem).wait()


def part(both, u_out, v_out, sems):
    copies = [pltpu.make_async_copy(both.at[k], out, sems.at[k]) for k, out in enumerate((u_out, v_out))]
    for copy in copies:
        copy.start()
    for copy in copies:
        copy.wait()


def shards(displacement, velocity, body_force, modulus, damage_bits):
    rows = NZ * NY
    vmem = pltpu.VMEM
    dma = pltpu.SemaphoreType.DMA
    block = (NZ, NX)
    anywhere = pl.BlockSpec(memory_space=pl.ANY)
    out = jax.ShapeDtypeStruct((3, rows, NX), F32)
    both = pl.pallas_call(
        kernel,
        name="relax",
        out_shape=vmem((2, 3, rows, NX), F32),
        in_specs=[anywhere] * 5,
        out_specs=pl.BlockSpec(memory_space=vmem),
        scratch_shapes=[
            vmem((3, rows, NX), F32), vmem((3, rows, NX), F32), vmem((3, rows, NX), F32),
            vmem((rows, NX), F32), vmem((2, rows, NX), jnp.int32),
                        vmem((9, 2, 3, ROWS) + block, F32),
            vmem((2, 3, ROWS) + block, F32),
            vmem((2, 3, ROWS) + block, F32),
            vmem((8, 2, 2, 3, ROWS) + block, F32),
            vmem((8, 2, 2, 2, ROWS) + block, F32),
            vmem((2, len(FULL), NY + 4) + block, F32),
            vmem((2, 25) + block, F32),
            vmem((5, 2) + block, F32),
            vmem((5, 6, 2) + block, F32),
            vmem((SLOTS,) + block, F32),
            vmem((2, 8, NX), F32),
            vmem((GX, NX), F32),
            vmem((GY * GZ, NX), F32),
            dma((5,)),
            dma((6, 4)), dma((6, 4)),
            dma((3, 6)), dma((3, 6)),
            dma, dma, dma, dma,
            pltpu.SemaphoreType.REGULAR((2,)),
        ],
        compiler_params=pltpu.CompilerParams(
            collective_id=0, has_side_effects=True, vmem_limit_bytes=60 * 1024 * 1024
        ),
    )(
        displacement.reshape(3, rows, NX),
        velocity.reshape(3, rows, NX),
        body_force.reshape(3, rows, NX),
        modulus.reshape(rows, NX),
        damage_bits.reshape(2, rows, NX),
    )
    u, v = pl.pallas_call(
        part,
        name="part",
        out_shape=(out, out),
        in_specs=[pl.BlockSpec(memory_space=vmem)],
        out_specs=(anywhere, anywhere),
        scratch_shapes=[dma((2,))],
        compiler_params=pltpu.CompilerParams(vmem_limit_bytes=1024 * 1024),
    )(both)
    return u.reshape(displacement.shape), v.reshape(velocity.shape)


def solution(mesh):
    placed = (
        P(None, None, "gy", "gx"),
        P(None, None, "gy", "gx"),
        P(None, None, "gy", "gx"),
        P(None, "gy", "gx"),
        P(None, None, "gy", "gx"),
    )
    return jax.shard_map(
        shards,
        mesh=mesh,
        in_specs=placed,
        out_specs=(P(None, None, "gy", "gx"), P(None, None, "gy", "gx")),
        check_vma=False,
    )
```

```python
import functools
import math

import jax
import jax.numpy as jnp
from jax import lax
from jax.experimental import pallas as pl
from jax.experimental.pallas import tpu as pltpu
from jax.sharding import PartitionSpec as P

ITERS = 4
NZ, NY, NX = 8, 8, 128
GX, GY, GZ = 16, 8, 8
MESH = pl.DeviceIdType.MESH
F32 = jnp.float32


def half_offsets():
    result = []
    for step_x in range(-2, 3):
        for step_y in range(-2, 3):
            for step_z in range(-2, 3):
                length_sq = step_x * step_x + step_y * step_y + step_z * step_z
                leading = step_x if step_x != 0 else step_y if step_y != 0 else step_z
                if 0 < length_sq <= 4 and leading > 0:
                    result.append((step_x, step_y, step_z))
    return result


HALF = half_offsets()
FULL = [(entry, number, 1) for number, entry in enumerate(HALF)] + [
    (tuple(-part for part in entry), number, -1) for number, entry in enumerate(HALF)
]
BOND = {entry: place for place, (entry, _, _) in enumerate(FULL)}
FICTIVE_MASS = 2.0 * sum(1.0 / math.sqrt(a * a + b * b + c * c) for a, b, c in HALF)

SIDES = [(-1, 0), (1, 0), (-1, -1), (1, -1), (-1, 1), (1, 1)]


def hops(distance, count):
    return min(distance % count, -distance % count)


CHIPS = GX // 2
X_STEPS = sorted(range(CHIPS), key=lambda d: -hops(d, CHIPS))
YZ_STEPS = sorted(
    [(dy, dz) for dy in range(GY) for dz in range(GZ) if dy or dz],
    key=lambda d: -(hops(d[0], GY) + hops(d[1], GZ)),
)

U, V0, G0, V1, G1, V2, G2, V3, G3 = range(9)
CHAIN_V, CHAIN_G = (V0, V1, V2, V3), (G0, G1, G2, G3)
EARLY = [(V0, V0), (V0, V1), (V1, V1), (G0, G0), (G0, G1), (G1, G1), (V0, G0), (V1, G0), (V1, G1)]
MIDDLE = [(V1, V2), (V2, V2), (V2, V3), (V2, G1)]
LATE = [(G1, G2), (G2, G2), (V2, G2), (V3, G2), (G2, G3)]
PAIRS = EARLY + MIDDLE + LATE
SLOTS = 24


def moment_slots(first, second):
    return [
        PAIRS.index(next((first[i], second[k - i]) for i in range(4) if 0 <= k - i < 4 and (first[i], second[k - i]) in PAIRS))
        for k in range(6)
    ]


VV, GG, VG = moment_slots(CHAIN_V, CHAIN_V), moment_slots(CHAIN_G, CHAIN_G), moment_slots(CHAIN_V, CHAIN_G)
REACH = 4
ROWS = NY + 2 * REACH


def kernel(
    u_hbm, v_hbm, body_hbm, mod_hbm, bits_hbm, result,
    raw_u, raw_v, raw_body, raw_mod, raw_bits,
    field, static, force, near_x, far_x, stiff, weights, edge_out, edge_in, moments, row_out, row_x, row_yz,
    load_sem, y_send, y_recv, side_send, side_recv, rx_send, rx_recv, ryz_send, ryz_recv, known,
):
    gx, gy = lax.axis_index("gx"), lax.axis_index("gy")
    part_y, part_z, core = gy // GZ, gy % GZ, gx % 2

    def near(dx, dy):
        return ((gx + dx + GX) % GX, (gy + dy + GY * GZ) % (GY * GZ))

    def across(dy, dz):
        return ((part_y + dy) % GY) * GZ + (part_z + dz) % GZ

    greeted = [near(dx, dy) for dx in (-1, 0, 1) for dy in (-1, 0, 1) if dx or dy]
    x_partners = [((gx + d) % GX, gy) for d in sorted(range(1, GX), key=lambda d: -hops(d, GX))]
    yz_partners = [(gx, across(dy, dz)) for dy, dz in YZ_STEPS]
    greeted += [near(dx, 0) for dx in (-2, 2)]
    boxes = [(dy, dz) for dy in (-1, 0, 1) for dz in (-1, 0, 1) if dy or dz]
    greeted += [(gx, across(dy, dz)) for dy, dz in boxes]
    rounds = [
        [near(dx * k, 0) for dx in (-2, 2)] + [(gx, across(dy * k, dz * k)) for dy, dz in boxes]
        for k in (1, 2)
    ]

    def call(number):
        for device in rounds[number]:
            pl.semaphore_signal(known.at[number], inc=1, device_id=device, device_id_type=MESH)

    def heard(number):
        pl.semaphore_wait(known.at[number], len(rounds[number]))

    barrier = pltpu.get_barrier_semaphore()

    def greet(devices):
        for device in devices:
            pl.semaphore_signal(barrier, inc=1, device_id=device, device_id_type=MESH)

    loads = [
        pltpu.make_async_copy(source, target, load_sem.at[place])
        for place, (source, target) in enumerate(
            [(u_hbm, raw_u), (mod_hbm, raw_mod), (bits_hbm, raw_bits), (v_hbm, raw_v), (body_hbm, raw_body)]
        )
    ]
    for load in loads:
        load.start()
    greet(greeted)

    lane = lax.broadcasted_iota(jnp.int32, (NZ, NX), 1)
    layer = lax.broadcasted_iota(jnp.int32, (NZ, NX), 0)
    nothing = jnp.zeros((NZ, NX), F32)

    def lanes_on(value, amount):
        return pltpu.roll(value, (-amount) % NX, axis=1)

    def layers_on(value, amount):
        return value if amount == 0 else pltpu.roll(value, (-amount) % NZ, axis=0)

    def plus(value, other, amount):
        if amount > 0:
            return lanes_on(jnp.where(lane < amount, other, value), amount)
        return lanes_on(jnp.where(lane >= NX + amount, other, value), amount)

    def pack(values, width, start=0):
        total = nothing
        for place, value in enumerate(values):
            turned = pltpu.roll(value, (8 * place + start + width) % NX, axis=1)
            total = jnp.where(lane // 8 == place, turned, total)
        return total

    def remote(source, target, send, recv, device):
        return pltpu.make_async_remote_copy(
            src_ref=source, dst_ref=target, send_sem=send, recv_sem=recv,
            device_id=device, device_id_type=MESH,
        )

    def row_copies(number):
        ref, deep, up, down = [
            (static.at[0], 4, slice(0, 2), slice(0, 1)),
            (field.at[U, 0], 4, slice(1, 2), slice(1, 2)),
            (field.at[V0, 0], 2, slice(1, 2), slice(1, 2)),
            (force.at[0], 2, slice(1, 2), slice(1, 2)),
            (field.at[V1, 0], 4, slice(1, 2), slice(1, 2)),
            (field.at[G1, 0], 4, slice(1, 2), slice(1, 2)),
        ][number]
        top, low = REACH + NY, REACH
        spans = [
            (slice(0, 3), slice(top - deep + 1, top), slice(low - deep + 1, low), 1),
            (slice(0, 3), slice(low, low + deep - 1), slice(top, top + deep - 1), -1),
            (up, slice(top - deep, top - deep + 1), slice(low - deep, low - deep + 1), 1),
            (down, slice(low + deep - 1, low + deep), slice(top + deep - 1, top + deep), -1),
        ]
        return [
            remote(ref.at[what, source], ref.at[what, target], y_send.at[number, place], y_recv.at[number, place], near(0, way))
            for place, (what, source, target, way) in enumerate(spans)
        ]

    def side_copies(group):
        first, last = [(0, 3), (3, 4), (4, 5)][group]
        copies = []
        for place, (dx, dy) in enumerate(SIDES):
            half = slice(0, 2) if dy == 0 else slice(1, 2) if dy < 0 else slice(0, 1)
            copies.append(
                remote(
                    edge_out.at[first:last, half], edge_in.at[first:last, place, half],
                    side_send.at[group, place], side_recv.at[group, place], near(-dx, -dy),
                )
            )
        return copies

    for load in loads:
        load.wait()
    for y in range(NY):
        turned = pl.ds(y, NZ, stride=NY)
        for c in range(3):
            field[U, 0, c, REACH + y] = raw_u[c, turned, :]
            field[V0, 0, c, REACH + y] = raw_v[c, turned, :]
            force[0, c, REACH + y] = raw_body[c, turned, :]
        static[0, 0, REACH + y] = raw_mod[turned, :]
        for c in range(2):
            static[0, 1 + c, REACH + y] = raw_bits[c, turned, :].astype(F32)

    def rows_of(ref, half):
        return [ref[c, REACH + 4 * half + y] for y in range(4) for c in range(3)]

    for half in range(2):
        edge_out[0, half] = pack(rows_of(static.at[0], half), 4)
        edge_out[1, half] = pack(rows_of(field.at[U, 0], half), 4)
        edge_out[2, half] = jnp.where(
            lane % 8 < 4, pack(rows_of(field.at[V0, 0], half), 2), pack(rows_of(force.at[0], half), 2, 4)
        )

    pl.semaphore_wait(barrier, len(greeted))
    for number in range(4):
        for copy in row_copies(number):
            copy.start()
        if number == 0:
            for copy in side_copies(0):
                copy.start()
    call(0)

    def unpack(ref, number, half, sides, first, width, start=0, depth=4):
        both = jnp.where(
            lane % (2 * width) < width, edge_in[number, sides, half], edge_in[number, sides + 1, half]
        )
        for y in range(4):
            if first < 0 and y < 4 - depth or first >= NY and y >= depth:
                continue
            for c in range(3):
                slot = 8 * (3 * y + c) + start + width
                ref[c, REACH + first + y] = pltpu.roll(both, (2 * NX - slot) % NX, axis=1)

    def shift(value_ref, slot, rows, far_rows, kinds=(0, 1), comps=(0, 1, 2), ahead=(0, 1, 2), far=((0, 0, 0), (1, 0, 0))):
        for y in rows:
            row = REACH + y
            for e in kinds:
                for c in comps:
                    value, other = value_ref[e, c, row], value_ref[1 - e, c, row]
                    if c in ahead:
                        near_x[slot, e, 0, c, row] = plus(value, other, 1)
                    near_x[slot, e, 1, c, row] = plus(value, other, -1)
                    for way, which, place in far:
                        if which == c and y in far_rows:
                            far_x[slot, e, way, place, row] = plus(value, other, 2 - 4 * way)

    columns = {0: lane, 1: jnp.where(lane < NX // 2, lane + NX, lane - NX)}
    for e in range(2):
        for a in range(-2, 3):
            there = columns[e] + a
            on = jnp.logical_and(jnp.logical_or(gx > 0, there >= 0), jnp.logical_or(gx < GX - 1, there < NX))
            for c in range(-2, 3):
                if a * a + c * c <= 4:
                    inside = jnp.logical_and(layer + c >= 0, layer + c < NZ)
                    weights[e, 5 * (a + 2) + c + 2] = jnp.logical_and(on, inside).astype(F32)

    def stiff_row(y, kinds=(0, 1)):
        row_on = {}
        for b in range(-2, 3):
            on = jnp.logical_and(
                jnp.logical_or(gy > 0, y + b >= 0), jnp.logical_or(gy < GY * GZ - 1, y + b < NY)
            )
            row_on[b] = jnp.where(on, 1.0, 0.0).astype(F32)
        for e in kinds:

            def at(c, a, b):
                row = REACH + y + b
                if a == 0:
                    return static[e, c, row]
                if abs(a) == 1:
                    return near_x[0, e, 0 if a > 0 else 1, c, row]
                return far_x[0, e, 0 if a > 0 else 1, 0 if c == 0 else 1, row]

            own = static[e, 0, REACH + y]
            words, partners, values = {}, {}, []
            for (a, b, c), number, sign in FULL:
                if (a, b, c) not in partners:
                    partners[a, b, c] = layers_on(at(0, a, b), c)
                length_sq = a * a + b * b + c * c
                scale = 0.5 / (length_sq * math.sqrt(length_sq)) * (4.0 if length_sq == 4 else 1.0)
                value = (own + partners[a, b, c]) * (weights[e, 5 * (a + 2) + c + 2] * (row_on[b] * scale))
                where = (number // 8, a, b) if sign < 0 else (number // 8, 0, 0)
                if where not in words:
                    words[where] = at(1 + where[0], where[1], where[2]).astype(jnp.int32)
                broken = jnp.bitwise_and(words[where], 1 << (number % 8))
                if sign < 0:
                    broken = layers_on(broken, c)
                values.append(jnp.where(broken == 0, value, 0.0))
            for place, value in enumerate(values):
                stiff[e, place, 2 + y] = value

    def pull(f, slot, e, y):
        row = REACH + y
        own = [field[f, e, c, row] for c in range(3)]
        total = [nothing, nothing, nothing]

        def bond(a, b, c):
            return stiff[e, BOND[a, b, c], 2 + y]

        for c in (-1, 1, -2, 2):
            total[2] += bond(0, 0, c) * (layers_on(own[2], c) - own[2])
        for b in (-1, 1):
            pair = [None if c == 0 else field[f, e, c, row + b] for c in range(3)]
            pulls = {}
            for gamma in (-1, 0, 1):
                c = gamma * b
                partner = pair[1] + gamma * pair[2] if gamma else pair[1]
                mine = own[1] + gamma * own[2] if gamma else own[1]
                pulls[gamma] = bond(0, b, c) * (layers_on(partner, c) - mine)
            total[1] += pulls[-1] + pulls[0] + pulls[1]
            total[2] += pulls[1] - pulls[-1]
        for b in (-2, 2):
            total[1] += bond(0, b, 0) * (field[f, e, 1, row + b] - own[1])
        for way in range(2):
            total[0] += bond(2 - 4 * way, 0, 0) * (far_x[slot, e, way, 0, row] - own[0])
        for beta in (-1, 0, 1):
            mine = own[0] + beta * own[1] if beta else own[0]
            for way, a in enumerate((1, -1)):
                b = a * beta
                pair = [near_x[slot, e, way, c, row + b] for c in range(3)]
                partner = pair[0] + beta * pair[1] if beta else pair[0]
                pulls = {}
                for gamma in (-1, 0, 1):
                    c = gamma * a
                    there = partner + gamma * pair[2] if gamma else partner
                    here = mine + gamma * own[2] if gamma else mine
                    pulls[gamma] = bond(a, b, c) * (layers_on(there, c) - here)
                both = pulls[-1] + pulls[0] + pulls[1]
                total[0] += both
                if beta:
                    total[1] += beta * both
                total[2] += pulls[1] - pulls[-1]
        return total

    def advance(f, slot, to, kinds, y):
        row = REACH + y
        news = [pull(f, slot, e, y) for e in kinds]
        if to == G0:
            news = [[new[c] + force[e, c, row] for c in range(3)] for e, new in zip(kinds, news)]
        for e, new in zip(kinds, news):
            for c in range(3):
                field[to, e, c, row] = new[c]

    def loop(count, where, *work):
        def one(index, carry):
            y = where(index)
            for step in work:
                step(y)
            return carry

        lax.fori_loop(0, count, one, 0)

    def inner(index):
        return index + 2

    def outer(index):
        return index - 1 + 4 * (index // 3)

    def ends(index):
        return 11 * index - 2

    def rim(index):
        return index + 4 * (index // 2)

    def all_rows(index):
        return index

    def dot(first, second):
        return first[0] * second[0] + first[1] * second[1] + first[2] * second[2]

    def gather(pairs, last_step=None):
        used = sorted({f for pair in pairs for f in pair})

        def row(y, sums):
            if last_step is not None:
                last_step(y)
            have = {f: [field[f, 0, c, REACH + y] for c in range(3)] for f in used}
            return tuple(total + dot(have[a], have[b]) for total, (a, b) in zip(sums, pairs))

        sums = lax.fori_loop(0, NY, row, (nothing,) * len(pairs))
        for pair, total in zip(pairs, sums):
            moments[PAIRS.index(pair)] = total

    own_rows, outside = list(range(NY)), [-3, -2, -1, 8, 9, 10]
    wide_rows = set(range(-2, NY + 2))

    def halves(ref, number, width, start=0, depth=4, sides=(0,)):
        if 0 in sides:
            unpack(ref, number, 0, 0, 0, width, start)
            unpack(ref, number, 1, 0, 4, width, start)
        else:
            unpack(ref, number, 1, 2, -4, width, start, depth)
            unpack(ref, number, 0, 4, NY, width, start, depth)

    def shift_static(rows):
        shift(static, 0, rows, wide_rows, ahead=(0,), far=((0, 0, 0), (1, 0, 0), (1, 2, 1)))

    for copy in side_copies(0)[:2]:
        copy.wait_recv()
    halves(static.at[1], 0, 4)
    halves(field.at[U, 1], 1, 4)
    halves(field.at[V0, 1], 2, 2)
    halves(force.at[1], 2, 2, 4)
    shift_static(own_rows)
    shift(field.at[U], 1, own_rows, wide_rows)
    shift(field.at[V0], 2, own_rows, set(own_rows), kinds=(0,))
    loop(4, inner, stiff_row)
    loop(4, inner, lambda y: advance(V0, 2, V1, (0,), y), lambda y: advance(U, 1, G0, (0, 1), y))
    heard(0)
    call(1)
    for copy in side_copies(0)[2:] + row_copies(0):
        copy.wait_recv()
    halves(static.at[1], 0, 4, sides=(1,))
    halves(field.at[U, 1], 1, 4, sides=(1,))
    halves(field.at[V0, 1], 2, 2, depth=1, sides=(1,))
    halves(force.at[1], 2, 2, 4, depth=2, sides=(1,))
    shift_static(outside)
    loop(6, outer, stiff_row)
    loop(2, ends, lambda y: stiff_row(y, (0,)))
    for copy in row_copies(1) + row_copies(2):
        copy.wait_recv()
    shift(field.at[V0], 2, [-1, 8], set(), kinds=(0,))
    shift(field.at[U], 1, outside, wide_rows)
    loop(4, rim, lambda y: advance(V0, 2, V1, (0,), y))
    for copy in row_copies(4):
        copy.start()
    for half in range(2):
        edge_out[3, half] = pack(rows_of(field.at[V1, 0], half), 4)
    for copy in side_copies(1):
        copy.start()
    for copy in row_copies(3):
        copy.wait_recv()
    loop(6, outer, lambda y: advance(U, 1, G0, (0, 1), y))
    loop(2, ends, lambda y: advance(U, 1, G0, (0,), y))
    shift(field.at[G0], 3, [-1] + own_rows + [8], set(own_rows), kinds=(0,))
    loop(4, rim, lambda y: advance(G0, 3, G1, (0,), y))
    loop(4, inner, lambda y: advance(G0, 3, G1, (0,), y))
    for copy in row_copies(5):
        copy.start()
    for half in range(2):
        edge_out[4, half] = pack(rows_of(field.at[G1, 0], half), 4)
    for copy in side_copies(2):
        copy.start()

    gather(EARLY)
    for copy in side_copies(1)[:2]:
        copy.wait_recv()
    halves(field.at[V1, 1], 3, 4)
    shift(field.at[V1], 4, own_rows, wide_rows)
    loop(4, inner, lambda y: advance(V1, 4, V2, (0, 1), y))
    for copy in side_copies(2)[:2]:
        copy.wait_recv()
    halves(field.at[G1, 1], 4, 4)
    shift(field.at[G1], 6, own_rows, wide_rows)
    loop(4, inner, lambda y: advance(G1, 6, G2, (0, 1), y))
    for copy in side_copies(1)[2:] + row_copies(4):
        copy.wait_recv()
    halves(field.at[V1, 1], 3, 4, sides=(1,))
    shift(field.at[V1], 4, outside, wide_rows)
    loop(6, outer, lambda y: advance(V1, 4, V2, (0, 1), y))
    loop(2, ends, lambda y: advance(V1, 4, V2, (0,), y))
    shift(field.at[V2], 5, [-1] + own_rows + [8], set(own_rows), kinds=(0,))
    gather(MIDDLE, lambda y: advance(V2, 5, V3, (0,), y))
    for copy in side_copies(2)[2:] + row_copies(5):
        copy.wait_recv()
    halves(field.at[G1, 1], 4, 4, sides=(1,))
    shift(field.at[G1], 6, outside, wide_rows)
    loop(6, outer, lambda y: advance(G1, 6, G2, (0, 1), y))
    loop(2, ends, lambda y: advance(G1, 6, G2, (0,), y))
    shift(field.at[G2], 7, [-1] + own_rows + [8], set(own_rows), kinds=(0,))
    for place in range(len(PAIRS), SLOTS):
        moments[place] = nothing
    gather(LATE, lambda y: advance(G2, 7, G3, (0,), y))

    heard(1)
    wide_lane = lax.broadcasted_iota(jnp.int32, (SLOTS, NX), 1)
    wide_row = lax.broadcasted_iota(jnp.int32, (SLOTS, NX), 0)
    summed = jnp.sum(jnp.sum(moments[...], axis=1), axis=1, keepdims=True)
    flat = jnp.sum(jnp.where(wide_lane == wide_row, summed, 0.0), axis=0, keepdims=True)

    def exchange(value, rows, partners, out, send, recv):
        count = len(partners)
        row_out[out, 0:1] = value
        rows[count : count + 1] = value
        for place, device in enumerate(partners):
            remote(row_out.at[out, 0:1], rows.at[place : place + 1], send, recv, device).start()
        whole = rows.at[0:count]
        pltpu.make_async_copy(whole, whole, recv).wait()
        return jnp.sum(rows[...], axis=0, keepdims=True)

    flat = exchange(flat, row_x, x_partners, 0, rx_send, rx_recv)
    flat = exchange(flat, row_yz, yz_partners, 1, ryz_send, ryz_recv)

    spread = jnp.sum(jnp.where(wide_lane == wide_row, jnp.broadcast_to(flat, (SLOTS, NX)), 0.0), axis=1, keepdims=True)
    spread = jnp.broadcast_to(spread, (SLOTS, NX))
    vv, gg, vg = ([spread[place : place + 1] for place in places] for places in (VV, GG, VG))

    zero = jnp.zeros((1, NX), F32)
    one = jnp.ones((1, NX), F32)
    speed_v, speed_g = [one, zero, zero, zero], [zero] * 4
    pull_v, pull_g = [zero] * 4, [one, zero, zero, zero]
    path_v, path_g = [zero] * 4, [zero] * 4
    for n in range(ITERS):
        terms = range(n if n else 1)

        def quadratic(order):
            parts = []
            for total in range(2 * len(terms) - 1):
                pairs = [(i, total - i) for i in terms if total - i in terms]
                parts.append(sum(speed_v[i] * speed_v[j] for i, j in pairs) * vv[total + order])
                if n:
                    parts.append(sum(speed_v[i] * speed_g[j] for i, j in pairs) * (2.0 * vg[total + order]))
                    parts.append(sum(speed_g[i] * speed_g[j] for i, j in pairs) * gg[total + order])
            while len(parts) > 1:
                parts = [parts[k] + parts[k + 1] if k + 1 < len(parts) else parts[k] for k in range(0, len(parts), 2)]
            return parts[0]

        denominator = quadratic(0)
        numerator = jnp.maximum(-quadratic(1) / FICTIVE_MASS, 0.0)
        damping = 2.0 * jnp.sqrt(numerator / (denominator + 1e-06))
        keep = (2.0 - damping) / (2.0 + damping)
        gain = 2.0 / (FICTIVE_MASS * (2.0 + damping))
        speed_v = [keep * x + gain * y for x, y in zip(speed_v, pull_v)]
        speed_g = [keep * x + gain * y for x, y in zip(speed_g, pull_g)]
        path_v = [x + y for x, y in zip(path_v, speed_v)]
        path_g = [x + y for x, y in zip(path_g, speed_g)]
        pull_v = [pull_v[0]] + [pull_v[j] + speed_v[j - 1] for j in range(1, 4)]
        pull_g = [pull_g[0]] + [pull_g[j] + speed_g[j - 1] for j in range(1, 4)]

    factors = [[jnp.broadcast_to(x, (NZ, NX)) for x in group] for group in (speed_v, speed_g, path_v, path_g)]

    def finish_row(y, carry):
        turned, row = pl.ds(y, NZ, stride=NY), REACH + y
        for c in range(3):
            basis = [field[f, 0, c, row] for f in CHAIN_V + CHAIN_G]
            result[1, c, turned, :] = sum(w * x for w, x in zip(factors[0] + factors[1], basis))
            moved = sum(w * x for w, x in zip(factors[2] + factors[3], basis))
            result[0, c, turned, :] = field[U, 0, c, row] + moved
        return carry

    lax.fori_loop(0, NY, finish_row, 0)
    for number in range(6):
        for copy in row_copies(number):
            copy.wait_send()
    for group in range(3):
        for copy in side_copies(group):
            copy.wait_send()

    for rows, count, sem in ((row_x, len(x_partners), rx_send), (row_yz, len(yz_partners), ryz_send)):
        whole = rows.at[0:count]
        pltpu.make_async_copy(whole, whole, sem).wait()


def part(both, u_out, v_out, sems):
    copies = [pltpu.make_async_copy(both.at[k], out, sems.at[k]) for k, out in enumerate((u_out, v_out))]
    for copy in copies:
        copy.start()
    for copy in copies:
        copy.wait()


def shards(displacement, velocity, body_force, modulus, damage_bits):
    rows = NZ * NY
    vmem = pltpu.VMEM
    dma = pltpu.SemaphoreType.DMA
    block = (NZ, NX)
    anywhere = pl.BlockSpec(memory_space=pl.ANY)
    out = jax.ShapeDtypeStruct((3, rows, NX), F32)
    both = pl.pallas_call(
        kernel,
        name="relax",
        out_shape=vmem((2, 3, rows, NX), F32),
        in_specs=[anywhere] * 5,
        out_specs=pl.BlockSpec(memory_space=vmem),
        scratch_shapes=[
            vmem((3, rows, NX), F32), vmem((3, rows, NX), F32), vmem((3, rows, NX), F32),
            vmem((rows, NX), F32), vmem((2, rows, NX), jnp.int32),
                        vmem((9, 2, 3, ROWS) + block, F32),
            vmem((2, 3, ROWS) + block, F32),
            vmem((2, 3, ROWS) + block, F32),
            vmem((8, 2, 2, 3, ROWS) + block, F32),
            vmem((8, 2, 2, 2, ROWS) + block, F32),
            vmem((2, len(FULL), NY + 4) + block, F32),
            vmem((2, 25) + block, F32),
            vmem((5, 2) + block, F32),
            vmem((5, 6, 2) + block, F32),
            vmem((SLOTS,) + block, F32),
            vmem((2, 8, NX), F32),
            vmem((GX, NX), F32),
            vmem((GY * GZ, NX), F32),
            dma((5,)),
            dma((6, 4)), dma((6, 4)),
            dma((3, 6)), dma((3, 6)),
            dma, dma, dma, dma,
            pltpu.SemaphoreType.REGULAR((2,)),
        ],
        compiler_params=pltpu.CompilerParams(
            collective_id=0, has_side_effects=True, vmem_limit_bytes=60 * 1024 * 1024
        ),
    )(
        displacement.reshape(3, rows, NX),
        velocity.reshape(3, rows, NX),
        body_force.reshape(3, rows, NX),
        modulus.reshape(rows, NX),
        damage_bits.reshape(2, rows, NX),
    )
    u, v = pl.pallas_call(
        part,
        name="part",
        out_shape=(out, out),
        in_specs=[pl.BlockSpec(memory_space=vmem)],
        out_specs=(anywhere, anywhere),
        scratch_shapes=[dma((2,))],
        compiler_params=pltpu.CompilerParams(vmem_limit_bytes=1024 * 1024),
    )(both)
    return u.reshape(displacement.shape), v.reshape(velocity.shape)


def solution(mesh):
    placed = (
        P(None, None, "gy", "gx"),
        P(None, None, "gy", "gx"),
        P(None, None, "gy", "gx"),
        P(None, "gy", "gx"),
        P(None, None, "gy", "gx"),
    )
    return jax.shard_map(
        shards,
        mesh=mesh,
        in_specs=placed,
        out_specs=(P(None, None, "gy", "gx"), P(None, None, "gy", "gx")),
        check_vma=False,
    )
```
